256 devices in a mesh: blk: 8 (over z_hi, x), group: 2 (over core), tp: 16 (over y, z_lo).
Axes of the slice: x: 4, y: 4, z: 8 (z_hi: 2, z_lo: 4; z = z_hi * 4 + z_lo), core: 2. Of those that a mesh axis runs over, the one named last changes fastest.
Arguments:
- prompt_query: bfloat16 [2, 2048, 8192], P('group', 'blk', 'tp'), may hold values from -9 to 9
- context_cache: bfloat16 [2, 2, 2048, 1024], P('group', None, 'blk', 'tp'), may hold values from -4 to 4
- new_block_cache: bfloat16 [2, 2, 2048, 1024], P('group', None, 'blk', 'tp'), may hold values from -4 to 4
- block_offset: int32 [2], replicated, may hold values from 512 to 2048
- page_owner: int32 [2, 128, 1], P('group', 'blk'), may hold values from 0 to 15; in each aligned block of 16 rows (0 to 15, 16 to 31, ..., all dimensions but the last counted through in order) at most 2 rows name the same one
- step_query: bfloat16 [16, 4, 16, 8192], P(('blk', 'group'), None, None, 'tp'), may hold values from -9 to 9
- step_cache: bfloat16 [16, 4, 2, 16, 2048], P(('blk', 'group'), None, None, None, 'tp'), may hold values from -4 to 4
- row_cache: bfloat16 [16, 2, 16, 256, 2048], P(('blk', 'group'), None, None, None, 'tp'), may hold values from -4 to 4
- row_lengths: int32 [16, 16], P(('blk', 'group')), may hold values from 2 to 256
- out_weight: bfloat16 [8192, 8192], P('tp'), may hold values from -0.0625 to 0.0625
- residual: bfloat16 [16, 4, 16, 8192], P(('blk', 'group'), None, None, 'tp'), may hold values from -48 to 48
- norm_gain: bfloat16 [8192], P('tp'), may hold values from 0.5 to 1.5
Outputs:
- prefill_out: bfloat16 [2, 2048, 8192], P('group', 'blk', 'tp')
- page_pool: bfloat16 [16, 32, 2, 16, 2048], P(('blk', 'group'), None, None, None, 'tp')
- decode_out: bfloat16 [16, 4, 16, 8192], P(('blk', 'group'), None, None, 'tp')
The draws below stay inside these ranges and needn't reach their ends.
Inputs may be any that keep to these rules, and one draw needn't show every extreme that they name: `page_owner`: among the 16 pages of one blk index of a prompt, each instance is named at most 2 times.
All inputs are finite; a program needn't handle non-finite values.
Results may differ from the reference program's by a relative error of at most 0.0029.
Values may be sent and summed in bfloat16 or wider, within the bound.
No kernel may reach another device: no remote copies, remote signals or barrier semaphores. Data moves between devices by JAX's collectives and lax.ppermute only.
A program may use at most 64 MiB of HBM per device.

```python
import math
import jax
import jax.numpy as jnp
import numpy as np
from jax import lax

D = 8192
QUERY_HEADS = 64
KEY_VALUE_HEADS = 8
HEAD_SIZE = 128
PAGE_TOKENS = 16
STEPS = 4
ROWS = 16
LEN = 256
BLOCK_TOKENS = 2048
CONTEXT_TOKENS = 2048
BLOCK_PAGES = 128
PAGES_DEV = 16
INST = 16
CAP = 2
SLOTS = 32
N_GROUP = 2
N_TP = 16


def draw_prompt_query(key, part):
    key = jax.random.fold_in(key, 1)
    array_shape = (N_GROUP, BLOCK_TOKENS, QUERY_HEADS * HEAD_SIZE)
    values = jnp.clip(jax.random.normal(key, array_shape, jnp.float32), -4.0, 4.0)
    return values.astype(jnp.bfloat16)


def draw_context_cache(key, part):
    key = jax.random.fold_in(key, 2)
    array_shape = (N_GROUP, 2, CONTEXT_TOKENS, KEY_VALUE_HEADS * HEAD_SIZE)
    values = jnp.clip(jax.random.normal(key, array_shape, jnp.float32), -4.0, 4.0)
    return values.astype(jnp.bfloat16)


def draw_block_offset(key, part):
    key = jax.random.fold_in(key, 3)
    first_key, second_key = jax.random.split(key)
    starts = jax.random.randint(first_key, (N_GROUP,), CONTEXT_TOKENS // 4, CONTEXT_TOKENS + 1)
    chosen = jax.random.randint(second_key, (), 0, N_GROUP)
    return starts.at[chosen].set(CONTEXT_TOKENS).astype(jnp.int32)


def draw_step_query(key, part):
    key = jax.random.fold_in(key, 4)
    array_shape = (INST, STEPS, ROWS, QUERY_HEADS * HEAD_SIZE)
    values = jnp.clip(jax.random.normal(key, array_shape, jnp.float32), -4.0, 4.0)
    return values.astype(jnp.bfloat16)


def draw_row_cache(key, part):
    key = jax.random.fold_in(key, 5)
    array_shape = (INST, 2, ROWS, LEN, N_TP * HEAD_SIZE)
    values = jnp.clip(jax.random.normal(key, array_shape, jnp.float32), -4.0, 4.0)
    return values.astype(jnp.bfloat16)


def draw_row_lengths(key, part):
    key = jax.random.fold_in(key, 6)
    first_key, second_key, third_key = jax.random.split(key, 3)
    reach = jax.random.randint(first_key, (INST, 1), LEN // 4, LEN + 1)
    raw_values = jax.random.randint(second_key, (INST, ROWS), 0, 1 << 20)
    lengths = 2 + raw_values % (reach - 1)
    chosen = jax.random.randint(third_key, (), 0, INST * ROWS)
    flat = lengths.reshape(-1).at[chosen].set(LEN)
    return flat.reshape(INST, ROWS).astype(jnp.int32)


def draw_residual(key, part):
    key = jax.random.fold_in(key, 7)
    first_key, second_key, third_key = jax.random.split(key, 3)
    array_shape = (INST, STEPS, ROWS, D)
    columns = jnp.exp(jax.random.uniform(second_key, (D,), jnp.float32, math.log(0.3), math.log(3.0)))
    row_scale = jnp.exp(jax.random.uniform(third_key, (INST, STEPS, ROWS, 1), jnp.float32, math.log(0.4), math.log(4.0)))
    values = jnp.clip(jax.random.normal(first_key, array_shape, jnp.float32), -4.0, 4.0)
    return (values * columns * row_scale).astype(jnp.bfloat16)


def block_levels(key, dims, shards, smallest, largest):
    factor_of, own = 1.0, jax.random.fold_in(key, 6)
    for position, blocks in shards:
        heights = jnp.exp(jax.random.uniform(jax.random.fold_in(own, position), (blocks,), jnp.float32, smallest / len(shards), largest / len(shards)))
        factor_of = factor_of * jnp.repeat(heights, dims[position] // blocks).reshape([-1 if axis == position else 1 for axis in range(len(dims))])
    return factor_of


def shared_out(rng, own, number, rows, number_of, top, limit, slope):
    ranking = jax.random.permutation(rng, number_of)
    heavy_load, common = load_shares(number_of, rows * top, limit, slope, True), load_shares(number_of, rows * top, limit, slope, False)
    places = jnp.arange(number_of)

    def named(sizes, offset_by):
        used = int((sizes > 0).sum())
        fixed = max(1, used // 4)
        passed = fixed + (places - fixed + offset_by * (used - fixed)) % max(1, number_of - fixed)
        return jnp.zeros((number_of,), jnp.int32).at[ranking[jnp.where(places < fixed, places, passed)]].set(jnp.asarray(sizes, jnp.int32))

    sizes = jnp.where(number % 4 == 0, named(heavy_load, number // 4), named(common, number - number // 4 - 1))
    mixed = jax.random.permutation(jax.random.fold_in(own, 3), number_of)
    donor, receiver = mixed[0:number_of // 2 * 2:2], mixed[1:number_of // 2 * 2:2]
    slack = jnp.minimum(sizes[donor] - 1, limit - sizes[receiver]) // 2
    slack = jnp.where((donor == ranking[0]) | (receiver == ranking[0]) | (sizes[receiver] == 0), 0, jnp.maximum(slack, 0))
    passed = jax.random.randint(jax.random.fold_in(own, 4), (number_of // 2,), 0, 1 << 20) % (slack + 1)
    sizes = sizes.at[donor].add(-passed).at[receiver].add(passed)
    members = jnp.searchsorted(jnp.cumsum(sizes), jnp.arange(rows * top), side="right").astype(jnp.int32)
    table = members.reshape(top, rows).T
    table = table[jax.random.permutation(jax.random.fold_in(own, 1), rows)]
    offset_by = jax.random.randint(jax.random.fold_in(own, 2), (rows, 1), 0, top)
    return jnp.take_along_axis(table, (jnp.arange(top)[None, :] + offset_by) % top, axis=1)


def load_shares(count, total, most, lean, full):
    loads = [(1 << 20) // math.isqrt(rank ** lean) + 1 for rank in range(1, count + 1)]
    largest = most if full else min(most, max(-(-total // count), total * loads[0] // sum(loads)))
    least = 1 if total - largest >= count - 1 else 0
    counts, surplus = [largest] + [least] * (count - 1), total - largest - least * (count - 1)
    while surplus > 0:
        candidates = [i for i in range(1, count) if counts[i] < largest] or [i for i in range(1, count) if counts[i] < most]
        mass, budget = sum([loads[i] for i in candidates]), surplus
        for i in candidates:
            addition = min(most - counts[i], max(1, budget * loads[i] // mass), surplus)
            counts[i] = counts[i] + addition
            surplus = surplus - addition
    return np.array(counts)


def centred(key, extent, scale, most, shards=(), kind=jnp.bfloat16):
    values = jax.random.normal(key, extent, jnp.float32) * scale
    if len(shards) > 0:
        values = block_levels(key, extent, shards, -0.22, 0.18) * values
    return jnp.clip(values, min=-most, max=most).astype(kind)


def setup_inputs(seed: int = 0) -> dict:
    key_list = jax.random.split(jax.random.key(seed), 13)
    prompt_query = draw_prompt_query(jax.random.fold_in(key_list[12], 71), 0)
    context_cache = draw_context_cache(jax.random.fold_in(key_list[12], 71), 0)
    new_block_cache = centred(key_list[2], (N_GROUP, 2, BLOCK_TOKENS, KEY_VALUE_HEADS * HEAD_SIZE), 1.0, 4.0, ((0, 2), (2, 8), (3, 16)))
    block_offset = draw_block_offset(jax.random.fold_in(key_list[12], 71), 0)
    page_owner_keys = jax.random.split(jax.random.fold_in(key_list[4], 1), N_GROUP * BLOCK_PAGES // PAGES_DEV)
    page_owner_turns = jax.random.permutation(jax.random.fold_in(key_list[4], 3), N_GROUP * BLOCK_PAGES // PAGES_DEV)
    page_owner = jax.vmap(lambda own, number: shared_out(jax.random.fold_in(key_list[4], 2), own, number, PAGES_DEV, INST, 1, CAP, 2))(page_owner_keys, page_owner_turns).reshape((N_GROUP, BLOCK_PAGES, 1))
    step_query = draw_step_query(jax.random.fold_in(key_list[12], 71), 0)
    step_cache = centred(key_list[6], (INST, STEPS, 2, ROWS, N_TP * HEAD_SIZE), 1.0, 4.0, ((0, 16), (4, 16)))
    row_cache = draw_row_cache(jax.random.fold_in(key_list[12], 71), 0)
    row_lengths = draw_row_lengths(jax.random.fold_in(key_list[12], 71), 0)
    out_weight = centred(key_list[9], (QUERY_HEADS * HEAD_SIZE, D), (QUERY_HEADS * HEAD_SIZE) ** -0.5, 0.0625, ((0, 16),))
    residual = draw_residual(jax.random.fold_in(key_list[12], 71), 0)
    norm_gain = jnp.clip(1.0 + 0.1 * jax.random.normal(key_list[11], (D,), jnp.float32), 0.5, 1.5).astype(jnp.bfloat16)
    return {"prompt_query": prompt_query, "context_cache": context_cache, "new_block_cache": new_block_cache, "block_offset": block_offset, "page_owner": page_owner, "step_query": step_query, "step_cache": step_cache, "row_cache": row_cache, "row_lengths": row_lengths, "out_weight": out_weight, "residual": residual, "norm_gain": norm_gain}


LOW_SCORE = -1e+30
EPSILON = 1e-05

def prefill_prompt(query_rows, context_key_value, block_key_value, offset):
    query_group_size = QUERY_HEADS // KEY_VALUE_HEADS
    heads_query = jnp.transpose(query_rows.reshape(BLOCK_TOKENS, QUERY_HEADS, HEAD_SIZE), (1, 0, 2))
    joined_keys = jnp.concatenate([context_key_value[0], block_key_value[0]], axis=0).reshape(CONTEXT_TOKENS + BLOCK_TOKENS, KEY_VALUE_HEADS, HEAD_SIZE)
    joined_values = jnp.concatenate([context_key_value[1], block_key_value[1]], axis=0).reshape(CONTEXT_TOKENS + BLOCK_TOKENS, KEY_VALUE_HEADS, HEAD_SIZE)
    head_keys = jnp.repeat(jnp.transpose(joined_keys, (1, 0, 2)), query_group_size, axis=0)
    head_values = jnp.repeat(jnp.transpose(joined_values, (1, 0, 2)), query_group_size, axis=0)
    query_pos = jnp.arange(BLOCK_TOKENS, dtype=jnp.int32)
    context_pos = jnp.arange(CONTEXT_TOKENS, dtype=jnp.int32)
    open_context = jnp.broadcast_to((context_pos < offset)[None, :], (BLOCK_TOKENS, CONTEXT_TOKENS))
    open_block = query_pos[None, :] <= query_pos[:, None]
    allowed = jnp.concatenate([open_context, open_block], axis=1)

    def one_head(operands):
        query_head, key_head, value_head = operands
        scores = jnp.dot(query_head, key_head.T, preferred_element_type=jnp.float32) * HEAD_SIZE ** (-0.5)
        scores = jnp.where(allowed, scores, LOW_SCORE)
        maxima = lax.optimization_barrier(jnp.max(scores, axis=1, keepdims=True))
        weights = jnp.where(allowed, jnp.exp(scores - maxima), 0.0)
        totals = lax.optimization_barrier(jnp.sum(weights, axis=1, keepdims=True))
        mixed = jnp.dot(weights, value_head.astype(jnp.float32), precision=lax.Precision.HIGHEST, preferred_element_type=jnp.float32)
        return (mixed / totals).astype(jnp.bfloat16)
    outputs = lax.map(one_head, (heads_query, head_keys, head_values))
    return jnp.transpose(outputs, (1, 0, 2)).reshape(BLOCK_TOKENS, QUERY_HEADS * HEAD_SIZE)

def build_pool(new_block_cache, page_owner):
    head_repeat_count = N_TP // KEY_VALUE_HEADS
    page_index = jnp.arange(BLOCK_PAGES, dtype=jnp.int32)
    source_block = page_index // PAGES_DEV
    same_source = source_block[None, :] == source_block[:, None]
    before = page_index[None, :] < page_index[:, None]
    slots_all = []
    pages_all = []
    for prompt_index in range(N_GROUP):
        owners = page_owner[prompt_index, :, 0]
        matches = same_source & before & (owners[None, :] == owners[:, None])
        ranks = lax.optimization_barrier(jnp.sum(matches.astype(jnp.int32), axis=1))
        source = source_block * N_GROUP + prompt_index
        slots_all.append((owners * SLOTS + source * CAP + ranks).astype(jnp.int32))
        paged_cache = new_block_cache[prompt_index].reshape(2, BLOCK_PAGES, PAGE_TOKENS, KEY_VALUE_HEADS, HEAD_SIZE)
        paged_cache = jnp.repeat(paged_cache, head_repeat_count, axis=3).reshape(2, BLOCK_PAGES, PAGE_TOKENS, N_TP * HEAD_SIZE)
        pages_all.append(jnp.transpose(paged_cache, (1, 0, 2, 3)))
    flat_slots = jnp.concatenate(slots_all)
    flat_pages = jnp.concatenate(pages_all)
    pool = jnp.zeros((INST * SLOTS, 2, PAGE_TOKENS, N_TP * HEAD_SIZE), jnp.bfloat16).at[flat_slots].set(flat_pages)
    return pool.reshape(INST, SLOTS, 2, PAGE_TOKENS, N_TP * HEAD_SIZE)

def reference(prompt_query, context_cache, new_block_cache, block_offset, page_owner, step_query, step_cache, row_cache, row_lengths, out_weight, residual, norm_gain):
    prefill_list = []
    for prompt_index in range(N_GROUP):
        prefill_list.append(prefill_prompt(prompt_query[prompt_index], context_cache[prompt_index], new_block_cache[prompt_index], block_offset[prompt_index]))
    prefill_out = jnp.stack(prefill_list)
    page_pool = build_pool(new_block_cache, page_owner)
    per_tensor = QUERY_HEADS // N_TP
    scaling = HEAD_SIZE ** (-0.5)
    gain_wide = norm_gain.astype(jnp.float32)

    def decode_instance(operands):
        queries, step_pairs, cache_pair, lengths, residual_rows = operands
        live = jnp.arange(LEN, dtype=jnp.int32)[None, :] < lengths[:, None]
        old_keys = cache_pair[0].reshape(ROWS, LEN, N_TP, HEAD_SIZE).astype(jnp.float32)
        old_values = cache_pair[1].reshape(ROWS, LEN, N_TP, HEAD_SIZE).astype(jnp.float32)
        results = []
        for number in range(STEPS):
            query_now = queries[number].reshape(ROWS, N_TP, per_tensor, HEAD_SIZE).astype(jnp.float32)
            new_keys = step_pairs[:number + 1, 0].reshape(number + 1, ROWS, N_TP, HEAD_SIZE).astype(jnp.float32)
            new_values = step_pairs[:number + 1, 1].reshape(number + 1, ROWS, N_TP, HEAD_SIZE).astype(jnp.float32)
            score_old = jnp.einsum('rtqd,rltd->rtql', query_now, old_keys) * scaling
            score_old = jnp.where(live[:, None, None, :], score_old, LOW_SCORE)
            score_new = jnp.einsum('rtqd,srtd->rtqs', query_now, new_keys) * scaling
            maxima = jnp.maximum(lax.optimization_barrier(jnp.max(score_old, axis=-1)), lax.optimization_barrier(jnp.max(score_new, axis=-1)))[..., None]
            weight_old = jnp.where(live[:, None, None, :], jnp.exp(score_old - maxima), 0.0)
            weight_new = jnp.exp(score_new - maxima)
            totals = lax.optimization_barrier(jnp.sum(weight_old, axis=-1)) + lax.optimization_barrier(jnp.sum(weight_new, axis=-1))
            rounded_old = lax.optimization_barrier(weight_old.astype(jnp.bfloat16)).astype(jnp.float32)
            rounded_new = lax.optimization_barrier(weight_new.astype(jnp.bfloat16)).astype(jnp.float32)
            mixed = jnp.einsum('rtql,rltd->rtqd', rounded_old, old_values) + jnp.einsum('rtqs,srtd->rtqd', rounded_new, new_values)
            attended = (mixed / totals[..., None]).astype(jnp.bfloat16).reshape(ROWS, QUERY_HEADS * HEAD_SIZE)
            hidden = residual_rows[number].astype(jnp.float32) + jnp.dot(attended, out_weight, preferred_element_type=jnp.float32)
            mean_square = lax.optimization_barrier(jnp.mean(hidden * hidden, axis=-1, keepdims=True))
            results.append((hidden * lax.rsqrt(mean_square + EPSILON) * gain_wide).astype(jnp.bfloat16))
        return jnp.stack(results)
    decode_out = lax.map(decode_instance, (step_query, step_cache, row_cache, row_lengths, residual))
    return (prefill_out, page_pool, decode_out)
```

```python
import functools
import math

import jax
import jax.numpy as jnp
from jax import lax
from jax.experimental import pallas as pl
from jax.experimental.pallas import tpu as pltpu
from jax.sharding import PartitionSpec as P

HEAD_SIZE = 128
PAGE_TOKENS = 16
STEPS = 4
ROWS = 16
LEN = 256
HEADS = 4
TOKENS = 256
PAGES = TOKENS // PAGE_TOKENS
HALF = HEAD_SIZE // 2
PACKED = 4 * TOKENS // 2
CHUNK = 4 * TOKENS
TAIL = 16
COLUMNS = 8192
QUARTER = COLUMNS // 4
SHARE = COLUMNS // 16
LOW_SCORE = -1e30
EPSILON = 1e-05
F32 = jnp.float32
BF16 = jnp.bfloat16
LOG2_SCALE = math.log2(math.e) * HEAD_SIZE**-0.5
VMEM = pltpu.VMEM
SMEM = pltpu.SMEM
PARAMS = pltpu.CompilerParams(vmem_limit_bytes=48 * 1024 * 1024)


def spec(space=VMEM):
    return pl.BlockSpec(memory_space=space)


def shape(dims, dtype):
    return jax.ShapeDtypeStruct(dims, dtype)


def dot_t(a, b):
    return lax.dot_general(a, b, (((1,), (1,)), ((), ())), preferred_element_type=F32)


def dot(a, b):
    return lax.dot_general(a, b, (((1,), (0,)), ((), ())), preferred_element_type=F32)


def pack_kernel(owner_ref, context_ref, block_ref, out_ref):
    half = TOKENS // 2
    for number in range(4):
        source = context_ref if number < 2 else block_ref
        piece = source[0, number % 2]
        out_ref[number * half : (number + 1) * half, :] = jnp.concatenate(
            [piece[:half], piece[half:]], axis=1
        )
    owners = [owner_ref[p] for p in range(PAGES)]
    page = lax.broadcasted_iota(jnp.int32, (TAIL, HEAD_SIZE), 1) // PAGE_TOKENS
    page = page + lax.broadcasted_iota(jnp.int32, (TAIL, HEAD_SIZE), 0) * (HEAD_SIZE // PAGE_TOKENS)
    codes = jnp.full((TAIL, HEAD_SIZE), -1, jnp.int32)
    for p in range(PAGES):
        rank = jnp.int32(0)
        for q in range(p):
            rank = rank + (owners[q] == owners[p]).astype(jnp.int32)
        codes = jnp.where(page == p, owners[p] * 2 + rank, codes)
    out_ref[PACKED:, :] = codes.astype(F32).astype(BF16)


def pack(page_owner, context_cache, new_block_cache):
    return pl.pallas_call(
        pack_kernel,
        out_shape=shape((PACKED + TAIL, HEAD_SIZE), BF16),
        in_specs=[spec(SMEM), spec(), spec()],
        out_specs=spec(),
        name="pack",
    )(page_owner, context_cache, new_block_cache)


def join_kernel(mine_ref, other_ref, out_ref):
    odd = lax.axis_index("tp") % 2
    half = TOKENS // 2

    def write(first_ref, second_ref):
        for number in range(4):
            rows = slice(number * half, (number + 1) * half)
            first, second = first_ref[rows, :], second_ref[rows, :]
            out_ref[number * TOKENS : number * TOKENS + half, :] = jnp.concatenate(
                [first[:, :HALF], second[:, :HALF]], axis=1
            )
            out_ref[number * TOKENS + half : (number + 1) * TOKENS, :] = jnp.concatenate(
                [first[:, HALF:], second[:, HALF:]], axis=1
            )

    @pl.when(odd == 0)
    def _():
        write(mine_ref, other_ref)

    @pl.when(odd == 1)
    def _():
        write(other_ref, mine_ref)

    out_ref[CHUNK:, :] = mine_ref[PACKED:, :]


def join(mine, other):
    return pl.pallas_call(
        join_kernel,
        out_shape=shape((CHUNK + TAIL, HEAD_SIZE), BF16),
        in_specs=[spec(), spec()],
        out_specs=spec(),
        name="join",
    )(mine, other)


def attend_kernel(offsets, first, last, *refs):
    offset_ref, query_ref = refs[:2]
    count = len(offsets)
    chunks = refs[2 : 2 + count]
    refs = refs[2 + count :]
    if not first:
        top_in, sum_in = refs[:2]
        refs = refs[2:]
    if last:
        (out_ref,) = refs
    else:
        top_out, sum_out = refs
    blk = lax.axis_index("blk")
    offset = offset_ref[lax.axis_index("group")]
    lane = lax.broadcasted_iota(jnp.int32, (1, TOKENS), 1)
    ones = jnp.ones((2 * TOKENS, HEAD_SIZE), BF16)
    rows_causal = lax.broadcasted_iota(jnp.int32, (TOKENS, TOKENS), 0)
    keys_causal = lax.broadcasted_iota(jnp.int32, (TOKENS, TOKENS), 1)
    keys, values, bias = [], [], []
    for (flip, turn), chunk in zip(offsets, chunks):
        source = (blk // 4 + flip) % 2 * 4 + (blk % 4 + turn + 4) % 4
        bias.append(jnp.where(source * TOKENS + lane < offset, 0.0, LOW_SCORE))
        bias.append(jnp.where(source * TOKENS + 0 * lane <= blk * TOKENS, 0.0, LOW_SCORE))
        keys += [chunk[:TOKENS, :], chunk[2 * TOKENS : 3 * TOKENS, :]]
        values += [chunk[TOKENS : 2 * TOKENS, :], chunk[3 * TOKENS : 4 * TOKENS, :]]
    for head in range(HEADS):
        query = query_ref[0, :, head * HEAD_SIZE : (head + 1) * HEAD_SIZE]
        rows = slice(head * TOKENS, (head + 1) * TOKENS)
        if first:
            top = jnp.full((TOKENS, 1), LOW_SCORE, F32)
            total = jnp.zeros((TOKENS, 2 * HEAD_SIZE), F32)
        else:
            top = top_in[rows, :1]
            total = sum_in[rows, :]
        for number in range(count):
            scores = []
            for part in (2 * number, 2 * number + 1):
                score = dot_t(query, keys[part]) * LOG2_SCALE + bias[part]
                if offsets[number] == (0, 0) and part % 2 == 1:
                    score = jnp.where(keys_causal <= rows_causal, score, LOW_SCORE)
                scores.append(score)
            score = jnp.concatenate(scores, axis=1)
            top_now = jnp.maximum(top, jnp.max(score, axis=1, keepdims=True))
            weight = jnp.exp2(score - top_now)
            high = weight.astype(BF16)
            low = (weight - high.astype(F32)).astype(BF16)
            value = jnp.concatenate(
                [jnp.concatenate(values[2 * number : 2 * number + 2], axis=0), ones], axis=1
            )
            fresh = dot(high, value) + dot(low, value)
            if first and number == 0:
                total = fresh
            else:
                total = total * jnp.exp2(top - top_now) + fresh
            top = top_now
        if last:
            out_ref[0, :, head * HEAD_SIZE : (head + 1) * HEAD_SIZE] = (
                total[:, :HEAD_SIZE] / total[:, HEAD_SIZE:]
            ).astype(BF16)
        else:
            top_out[rows, :] = jnp.broadcast_to(top, (TOKENS, HEAD_SIZE))
            sum_out[rows, :] = total


def attend(block_offset, queries, chunks, offsets, state, last):
    first = state is None
    operands = [block_offset, queries, *chunks] + ([] if first else list(state))
    rows = HEADS * TOKENS
    if last:
        out = shape((1, TOKENS, HEADS * HEAD_SIZE), BF16)
    else:
        out = (shape((rows, HEAD_SIZE), F32), shape((rows, 2 * HEAD_SIZE), F32))
    pairs = rows * len(chunks) * 2 * TOKENS
    return pl.pallas_call(
        functools.partial(attend_kernel, offsets, first, last),
        out_shape=out,
        in_specs=[spec(SMEM)] + [spec()] * (len(operands) - 1),
        out_specs=spec() if last else (spec(), spec()),
        compiler_params=PARAMS,
        cost_estimate=pl.CostEstimate(
            flops=pairs * HEAD_SIZE * 10, bytes_accessed=2 << 20, transcendentals=pairs
        ),
        name="attend",
    )(*operands)


def pages_kernel(offsets, *refs):
    chunks, (mine_ref, other_ref) = refs[:-2], refs[-2:]
    blk = lax.axis_index("blk")
    instance = blk * 2 + lax.axis_index("group")
    other = blk * 2 + 1 - lax.axis_index("group")
    slots = 4 * PAGE_TOKENS
    row = lax.broadcasted_iota(jnp.int32, (slots, TOKENS), 0)
    token = lax.broadcasted_iota(jnp.int32, (slots, TOKENS), 1)
    wanted = jnp.where(row < 2 * PAGE_TOKENS, instance * 2, other * 2) + row // PAGE_TOKENS % 2
    wanted = jnp.where(row % PAGE_TOKENS == token % PAGE_TOKENS, wanted, -2).astype(F32)
    for (flip, turn), chunk in zip(offsets, chunks):
        source = (blk // 4 + flip) % 2 * 4 + (blk % 4 + turn + 4) % 4
        codes = chunk[CHUNK : CHUNK + TAIL, :].astype(F32)
        codes = jnp.concatenate([codes[0:1], codes[1:2]], axis=1)
        chooser = (wanted == codes).astype(BF16)
        for part in range(2):
            cache = chunk[(2 + part) * TOKENS : (3 + part) * TOKENS, :]
            found = dot(chooser, cache).astype(BF16)
            for rank in range(2):
                mine_ref[source, rank, part] = found[rank * PAGE_TOKENS : (rank + 1) * PAGE_TOKENS]
                other_ref[source, rank, part] = found[
                    (2 + rank) * PAGE_TOKENS : (3 + rank) * PAGE_TOKENS
                ]


def select_pages(chunks, offsets):
    out = shape((8, 2, 2, PAGE_TOKENS, HEAD_SIZE), BF16)
    return pl.pallas_call(
        functools.partial(pages_kernel, offsets),
        out_shape=(out, out),
        in_specs=[spec()] * len(chunks),
        out_specs=(spec(), spec()),
        compiler_params=PARAMS,
        name="pages",
    )(*chunks)


def pool_kernel(mine_ref, came_ref, out_ref):
    group = lax.axis_index("group")
    out_ref[:, group] = mine_ref[...]
    out_ref[:, 1 - group] = came_ref[...]


def pool(mine, came):
    return pl.pallas_call(
        pool_kernel,
        out_shape=shape((8, 2, 2, 2, PAGE_TOKENS, HEAD_SIZE), BF16),
        in_specs=[spec(), spec()],
        out_specs=spec(),
        name="pool",
    )(mine, came)


def attend_rows(length_ref, query_ref, step_ref, cache_ref, attended_ref, score_ref, mixed_ref):
    count = HEADS * STEPS * ROWS
    query = jnp.concatenate(
        [
            query_ref[0, :, :, h * HEAD_SIZE : (h + 1) * HEAD_SIZE].reshape(STEPS * ROWS, HEAD_SIZE)
            for h in range(HEADS)
        ],
        axis=0,
    )
    scaling = HEAD_SIZE**-0.5

    def row_of(width):
        return lax.broadcasted_iota(jnp.int32, (count, width), 0) % ROWS

    row_wide, row_head = row_of(LEN), row_of(HEAD_SIZE)
    lengths = jnp.zeros((count, LEN), jnp.int32)
    for r in range(ROWS):
        score = dot_t(query, cache_ref[0, 0, r])
        if r == 0:
            score_ref[...] = score
        else:
            score_ref[...] = jnp.where(row_wide == r, score, score_ref[...])
        lengths = jnp.where(row_wide == r, length_ref[r], lengths)
    live = lax.broadcasted_iota(jnp.int32, (count, LEN), 1) < lengths
    score_old = jnp.where(live, score_ref[...] * scaling, LOW_SCORE)
    new_keys = step_ref[0, :, 0].reshape(STEPS * ROWS, HEAD_SIZE)
    new_values = step_ref[0, :, 1].reshape(STEPS * ROWS, HEAD_SIZE)
    lane = lax.broadcasted_iota(jnp.int32, (count, STEPS * ROWS), 1)
    place = lax.broadcasted_iota(jnp.int32, (count, STEPS * ROWS), 0)
    open_new = (lane % ROWS == place % ROWS) & (lane // ROWS <= place // ROWS % STEPS)
    score_new = jnp.where(open_new, dot_t(query, new_keys) * scaling, LOW_SCORE)
    top = jnp.maximum(
        jnp.max(score_old, axis=1, keepdims=True), jnp.max(score_new, axis=1, keepdims=True)
    )
    weight_old = jnp.where(live, jnp.exp(score_old - top), 0.0)
    weight_new = jnp.where(open_new, jnp.exp(score_new - top), 0.0)
    totals = jnp.sum(weight_old, axis=1, keepdims=True) + jnp.sum(weight_new, axis=1, keepdims=True)
    rounded = weight_old.astype(BF16)
    for r in range(ROWS):
        mixed = dot(rounded, cache_ref[0, 1, r])
        if r == 0:
            mixed_ref[...] = mixed
        else:
            mixed_ref[...] = jnp.where(row_head == r, mixed, mixed_ref[...])
    mixed = mixed_ref[...] + dot(weight_new.astype(BF16), new_values)
    attended = (mixed / totals).astype(BF16)
    for h in range(HEADS):
        attended_ref[:, h * HEAD_SIZE : (h + 1) * HEAD_SIZE] = attended[
            h * STEPS * ROWS : (h + 1) * STEPS * ROWS
        ]


TILES = 2


def decode_kernel(
    y_ref, length_ref, query_ref, step_ref, cache_ref, weight_ref, *refs
):
    outs, (attended_ref, score_ref, mixed_ref) = refs[:4], refs[4:]
    number = pl.program_id(0)

    @pl.when(number == 0)
    def _():
        attend_rows(length_ref, query_ref, step_ref, cache_ref, attended_ref, score_ref, mixed_ref)

    part = dot(attended_ref[...], weight_ref[...])
    for place, out in enumerate(outs):

        @pl.when(number // TILES == place)
        def _(out=out):
            out[...] = part.astype(out.dtype)


TURNS = (2, 1, 3, 0)


def decode(place, row_lengths, step_query, step_cache, row_cache, out_weight):
    width = QUARTER // TILES
    rows = STEPS * ROWS

    def weight_block(j, y):
        slot = j // TILES
        turn = jnp.where(slot == 0, 2, jnp.where(slot == 1, 1, jnp.where(slot == 2, 3, 0)))
        return (0, (y[0] + turn) % 4 * TILES + j % TILES)

    def whole(a):
        dims = a.shape
        return pl.BlockSpec(dims, lambda j, y: (0,) * len(dims))

    def out_block(slot):
        return pl.BlockSpec(
            (rows, width), lambda j, y: (0, jnp.clip(j - slot * TILES, 0, TILES - 1))
        )

    return pl.pallas_call(
        decode_kernel,
        out_shape=tuple(shape((rows, QUARTER), BF16 if t else F32) for t in TURNS),
        grid_spec=pltpu.PrefetchScalarGridSpec(
            num_scalar_prefetch=2,
            grid=(4 * TILES,),
            in_specs=[
                whole(step_query),
                whole(step_cache),
                whole(row_cache),
                pl.BlockSpec((out_weight.shape[0], width), lambda j, y, l: weight_block(j, y)),
            ]
            if False
            else [
                pl.BlockSpec(step_query.shape, lambda j, y, l: (0,) * 4),
                pl.BlockSpec(step_cache.shape, lambda j, y, l: (0,) * 5),
                pl.BlockSpec(row_cache.shape, lambda j, y, l: (0,) * 5),
                pl.BlockSpec((out_weight.shape[0], width), lambda j, y, l: weight_block(j, y)),
            ],
            out_specs=tuple(
                pl.BlockSpec(
                    (rows, width),
                    lambda j, y, l, s=s: (0, jnp.clip(j - s * TILES, 0, TILES - 1)),
                )
                for s in range(4)
            ),
            scratch_shapes=[
                pltpu.VMEM((rows, HEADS * HEAD_SIZE), BF16),
                pltpu.VMEM((HEADS * rows, LEN), F32),
                pltpu.VMEM((HEADS * rows, HEAD_SIZE), F32),
            ],
        ),
        compiler_params=PARAMS,
        cost_estimate=pl.CostEstimate(
            flops=2 * rows * 512 * COLUMNS, bytes_accessed=12 << 20, transcendentals=1 << 16
        ),
        name="decode",
    )(place, row_lengths, step_query, step_cache, row_cache, out_weight)


def quarter_kernel(own_ref, a_ref, b_ref, c_ref, *outs):
    z = lax.axis_index("tp") % 4
    for out, turn in zip(outs, TURNS):
        columns = pl.ds(pl.multiple_of((z + turn) % 4 * SHARE, SHARE), SHARE)
        out[...] = (
            own_ref[:, columns]
            + a_ref[:, columns].astype(F32)
            + b_ref[:, columns].astype(F32)
            + c_ref[:, columns].astype(F32)
        )


def sum_quarters(own, came):
    return pl.pallas_call(
        quarter_kernel,
        out_shape=tuple(shape((STEPS * ROWS, SHARE), F32) for _ in TURNS),
        in_specs=[spec()] * 4,
        out_specs=(spec(),) * 4,
        name="quarters",
    )(own, *came)


def hidden_kernel(residual_ref, own_ref, a_ref, b_ref, c_ref, hidden_ref, square_ref):
    residual = residual_ref[0].reshape(STEPS * ROWS, SHARE).astype(F32)
    hidden = residual + (own_ref[...] + a_ref[...] + b_ref[...] + c_ref[...])
    hidden_ref[...] = hidden
    square_ref[...] = jnp.broadcast_to(
        jnp.sum(hidden * hidden, axis=1, keepdims=True), square_ref.shape
    )


def sum_shares(residual, own, came):
    return pl.pallas_call(
        hidden_kernel,
        out_shape=(shape((STEPS * ROWS, SHARE), F32), shape((STEPS * ROWS, HEAD_SIZE), F32)),
        in_specs=[spec()] * 5,
        out_specs=(spec(), spec()),
        name="hidden",
    )(residual, own, *came)


def squares_kernel(own_ref, a_ref, b_ref, c_ref, out_ref):
    out_ref[...] = own_ref[...] + a_ref[...] + b_ref[...] + c_ref[...]


def sum_squares(own, came):
    return pl.pallas_call(
        squares_kernel,
        out_shape=shape((STEPS * ROWS, HEAD_SIZE), F32),
        in_specs=[spec()] * 4,
        out_specs=spec(),
        name="squares",
    )(own, *came)


def finish_kernel(hidden_ref, gain_ref, own_ref, a_ref, b_ref, c_ref, out_ref):
    square = own_ref[...] + a_ref[...] + b_ref[...] + c_ref[...]
    scale = lax.rsqrt(square * (1.0 / COLUMNS) + EPSILON)
    scale = jnp.concatenate([scale] * (SHARE // HEAD_SIZE), axis=1)
    out = hidden_ref[...] * scale * gain_ref[...].astype(F32)
    out_ref[0] = out.astype(BF16).reshape(STEPS, ROWS, SHARE)


def finish(hidden, gain, own, came):
    return pl.pallas_call(
        finish_kernel,
        out_shape=shape((1, STEPS, ROWS, SHARE), BF16),
        in_specs=[spec()] * 6,
        out_specs=spec(),
        name="finish",
    )(hidden, gain, own, *came)


def move_x(a, turn):
    return lax.ppermute(a, "blk", [(i, i // 4 * 4 + (i + turn) % 4) for i in range(8)])


def move_y(a, turn):
    return lax.ppermute(a, "tp", [(i, (i + 4 * turn) % 16) for i in range(16)])


def move_z(a, turn):
    return lax.ppermute(a, "tp", [(i, i // 4 * 4 + (i + turn) % 4) for i in range(16)])


def body(
    prompt_query,
    context_cache,
    new_block_cache,
    block_offset,
    page_owner,
    step_query,
    step_cache,
    row_cache,
    row_lengths,
    out_weight,
    residual,
    norm_gain,
):
    packed = pack(page_owner.reshape(PAGES), context_cache, new_block_cache)
    near = lax.ppermute(packed, "tp", [(i, i ^ 1) for i in range(16)])
    far = lax.ppermute(packed, "blk", [(i, i ^ 4) for i in range(8)])
    far_near = lax.ppermute(
        packed,
        ("blk", "tp"),
        [(b * 16 + t, (b ^ 4) * 16 + (t ^ 1)) for b in range(8) for t in range(16)],
    )
    place = (lax.axis_index("tp") // 4).astype(jnp.int32).reshape(1)
    parts = decode(
        place, row_lengths.reshape(ROWS), step_query, step_cache, row_cache, out_weight
    )
    came = [move_y(a, turn) for a, turn in zip(parts[:3], TURNS)]

    chunk = join(packed, near)
    chunk_far = join(far, far_near)
    up = move_x(chunk, 1)
    down = move_x(chunk, 3)
    far_up = move_x(chunk_far, 1)
    far_down = move_x(chunk_far, 3)
    up_two = move_x(up, 1)
    far_down_two = move_x(far_down, 3)

    state = attend(block_offset, prompt_query, [chunk, chunk_far], [(0, 0), (1, 0)], None, False)

    shares = sum_quarters(parts[3], came)
    came = [move_z(a, turn) for a, turn in zip(shares[:3], TURNS)]

    state = attend(
        block_offset,
        prompt_query,
        [up, down, far_up, far_down],
        [(0, -1), (0, 1), (1, -1), (1, 1)],
        state,
        False,
    )

    hidden, square = sum_shares(residual, shares[3], came)
    came = [move_y(square, turn) for turn in TURNS[:3]]
    square = sum_squares(square, came)
    came = [move_z(square, turn) for turn in TURNS[:3]]

    chunks = [chunk, chunk_far, up, down, far_up, far_down, up_two, far_down_two]
    offsets = [(0, 0), (1, 0), (0, -1), (0, 1), (1, -1), (1, 1), (0, 2), (1, 2)]
    mine, other = select_pages(chunks, offsets)
    other = lax.ppermute(other, "group", [(0, 1), (1, 0)])
    prefill_out = attend(
        block_offset, prompt_query, [up_two, far_down_two], [(0, 2), (1, 2)], state, True
    )
    page_pool = pool(mine, other).reshape(1, 32, 2, PAGE_TOKENS, HEAD_SIZE)
    decode_out = finish(hidden, norm_gain.reshape(1, SHARE), square, came)
    return (prefill_out, page_pool, decode_out)


def solution(mesh):
    placed = (
        P("group", "blk", "tp"),
        P("group", None, "blk", "tp"),
        P("group", None, "blk", "tp"),
        P(),
        P("group", "blk", None),
        P(("blk", "group"), None, None, "tp"),
        P(("blk", "group"), None, None, None, "tp"),
        P(("blk", "group"), None, None, None, "tp"),
        P(("blk", "group"), None),
        P("tp", None),
        P(("blk", "group"), None, None, "tp"),
        P("tp"),
    )
    return jax.shard_map(
        body,
        mesh=mesh,
        in_specs=placed,
        out_specs=(
            P("group", "blk", "tp"),
            P(("blk", "group"), None, None, None, "tp"),
            P(("blk", "group"), None, None, "tp"),
        ),
        check_vma=False,
    )
```

```python
import functools
import math

import jax
import jax.numpy as jnp
from jax import lax
from jax.experimental import pallas as pl
from jax.experimental.pallas import tpu as pltpu
from jax.sharding import PartitionSpec as P

HEAD_SIZE = 128
PAGE_TOKENS = 16
STEPS = 4
ROWS = 16
LEN = 256
HEADS = 4
TOKENS = 256
PAGES = TOKENS // PAGE_TOKENS
HALF = HEAD_SIZE // 2
PACKED = 4 * HALF
CHUNK = 4 * HEAD_SIZE
TAIL = 16
COLUMNS = 8192
QUARTER = COLUMNS // 4
SHARE = COLUMNS // 16
LOW_SCORE = -1e30
EPSILON = 1e-05
F32 = jnp.float32
BF16 = jnp.bfloat16
LOG2_SCALE = math.log2(math.e) * HEAD_SIZE**-0.5
VMEM = pltpu.VMEM
SMEM = pltpu.SMEM
MIB = 1024 * 1024


def params(mebibytes):
    return pltpu.CompilerParams(vmem_limit_bytes=mebibytes * MIB)


SMALL = pl.CostEstimate(flops=1024, bytes_accessed=1024, transcendentals=0)


def spec(space=VMEM):
    return pl.BlockSpec(memory_space=space)


def shape(dims, dtype):
    return jax.ShapeDtypeStruct(dims, dtype)


def dot_t(a, b):
    return lax.dot_general(a, b, (((1,), (1,)), ((), ())), preferred_element_type=F32)


def dot(a, b):
    return lax.dot_general(a, b, (((1,), (0,)), ((), ())), preferred_element_type=F32)


def pack_kernel(owner_ref, context_ref, block_ref, out_ref):
    for number in range(4):
        source = context_ref if number < 2 else block_ref
        out_ref[number * HALF : (number + 1) * HALF, :] = source[0, number % 2]
    owners = [owner_ref[p] for p in range(PAGES)]
    page = lax.broadcasted_iota(jnp.int32, (TAIL, TOKENS), 1) // PAGE_TOKENS
    codes = jnp.full((TAIL, TOKENS), -1, jnp.int32)
    for p in range(PAGES):
        rank = jnp.int32(0)
        for q in range(p):
            rank = rank + (owners[q] == owners[p]).astype(jnp.int32)
        codes = jnp.where(page == p, owners[p] * 2 + rank, codes)
    out_ref[PACKED:, :] = codes.astype(F32).astype(BF16)


def pack(page_owner, context_cache, new_block_cache):
    return pl.pallas_call(
        pack_kernel,
        out_shape=shape((PACKED + TAIL, TOKENS), BF16),
        in_specs=[spec(SMEM), spec(), spec()],
        out_specs=spec(),
        compiler_params=params(4),
        cost_estimate=SMALL,
        name="pack",
    )(page_owner, context_cache, new_block_cache)


def join_kernel(mine_ref, other_ref, after_ref, out_ref):
    odd = lax.axis_index("tp") % 2
    for number in range(4):
        rows = slice(number * HALF, (number + 1) * HALF)
        here = pl.multiple_of(number * HEAD_SIZE + odd * HALF, HALF)
        there = pl.multiple_of(number * HEAD_SIZE + (1 - odd) * HALF, HALF)
        out_ref[pl.ds(here, HALF), :] = mine_ref[rows, :]
        out_ref[pl.ds(there, HALF), :] = other_ref[rows, :]
    out_ref[CHUNK:, :] = mine_ref[PACKED:, :]


def join(mine, other, after):
    return pl.pallas_call(
        join_kernel,
        out_shape=shape((CHUNK + TAIL, TOKENS), BF16),
        in_specs=[spec(), spec(), spec(pl.ANY)],
        out_specs=spec(),
        compiler_params=params(4),
        cost_estimate=SMALL,
        name="join",
    )(mine, other, after)


def attend_kernel(offsets, first, last, *refs):
    offset_ref, query_ref = refs[:2]
    count = len(offsets)
    chunks = refs[2 : 2 + count]
    refs = refs[3 + count :]
    if not first:
        top_in, sum_in = refs[:2]
        refs = refs[2:]
    if last:
        (out_ref,) = refs
    else:
        top_out, sum_out = refs
    blk = lax.axis_index("blk")
    offset = offset_ref[lax.axis_index("group")]
    lane = lax.broadcasted_iota(jnp.int32, (1, TOKENS), 1)
    ones = jnp.ones((HEAD_SIZE, 2 * TOKENS), BF16)
    rows_causal = lax.broadcasted_iota(jnp.int32, (TOKENS, TOKENS), 0)
    keys_causal = lax.broadcasted_iota(jnp.int32, (TOKENS, TOKENS), 1)
    keys, values, bias = [], [], []
    for (flip, turn), chunk in zip(offsets, chunks):
        source = (blk // 4 + flip) % 2 * 4 + (blk % 4 + turn + 4) % 4
        bias.append(jnp.where(source * TOKENS + lane < offset, 0.0, LOW_SCORE))
        bias.append(jnp.where(source * TOKENS + 0 * lane <= blk * TOKENS, 0.0, LOW_SCORE))
        parts = [chunk[n * HEAD_SIZE : (n + 1) * HEAD_SIZE, :] for n in range(4)]
        keys += [parts[0], parts[2]]
        values.append(
            jnp.concatenate([jnp.concatenate([parts[1], parts[3]], axis=1), ones], axis=0)
        )
    for head in range(HEADS):
        query = query_ref[0, :, head * HEAD_SIZE : (head + 1) * HEAD_SIZE]
        rows = slice(head * TOKENS, (head + 1) * TOKENS)
        if first:
            top = jnp.full((TOKENS, 1), LOW_SCORE, F32)
            total = jnp.zeros((TOKENS, 2 * HEAD_SIZE), F32)
        else:
            top = top_in[rows, :1]
            total = sum_in[rows, :]
        for number in range(count):
            scores = []
            for part in (2 * number, 2 * number + 1):
                score = dot(query, keys[part]) * LOG2_SCALE + bias[part]
                if offsets[number] == (0, 0) and part % 2 == 1:
                    score = jnp.where(keys_causal <= rows_causal, score, LOW_SCORE)
                scores.append(score)
            score = jnp.concatenate(scores, axis=1)
            top_now = jnp.maximum(top, jnp.max(score, axis=1, keepdims=True))
            weight = jnp.exp2(score - top_now)
            high = weight.astype(BF16)
            low = (weight - high.astype(F32)).astype(BF16)
            fresh = dot_t(high, values[number]) + dot_t(low, values[number])
            if first and number == 0:
                total = fresh
            else:
                total = total * jnp.exp2(top - top_now) + fresh
            top = top_now
        if last:
            out_ref[0, :, head * HEAD_SIZE : (head + 1) * HEAD_SIZE] = (
                total[:, :HEAD_SIZE] / total[:, HEAD_SIZE:]
            ).astype(BF16)
        else:
            top_out[rows, :] = jnp.broadcast_to(top, (TOKENS, HEAD_SIZE))
            sum_out[rows, :] = total


def attend(block_offset, queries, chunks, offsets, state, last, after):
    first = state is None
    operands = [block_offset, queries, *chunks, after] + ([] if first else list(state))
    rows = HEADS * TOKENS
    if last:
        out = shape((1, TOKENS, HEADS * HEAD_SIZE), BF16)
    else:
        out = (shape((rows, HEAD_SIZE), F32), shape((rows, 2 * HEAD_SIZE), F32))
    return pl.pallas_call(
        functools.partial(attend_kernel, offsets, first, last),
        out_shape=out,
        in_specs=[spec(SMEM)]
        + [spec()] * (1 + len(chunks))
        + [spec(pl.ANY)]
        + [spec()] * (0 if first else 2),
        out_specs=spec() if last else (spec(), spec()),
        compiler_params=params(24),
        cost_estimate=SMALL,
        name="attend",
    )(*operands)


def pages_kernel(offsets, *refs):
    chunks, (mine_ref, other_ref) = refs[:-3], refs[-2:]
    blk = lax.axis_index("blk")
    instance = blk * 2 + lax.axis_index("group")
    other = blk * 2 + 1 - lax.axis_index("group")
    slots = 4 * PAGE_TOKENS
    row = lax.broadcasted_iota(jnp.int32, (slots, TOKENS), 0)
    token = lax.broadcasted_iota(jnp.int32, (slots, TOKENS), 1)
    wanted = jnp.where(row < 2 * PAGE_TOKENS, instance * 2, other * 2) + row // PAGE_TOKENS % 2
    wanted = jnp.where(row % PAGE_TOKENS == token % PAGE_TOKENS, wanted, -2).astype(F32)
    for (flip, turn), chunk in zip(offsets, chunks):
        source = (blk // 4 + flip) % 2 * 4 + (blk % 4 + turn + 4) % 4
        codes = chunk[CHUNK : CHUNK + TAIL, :].astype(F32)[0:1]
        chooser = jnp.where(wanted == codes, 1.0, 0.0).astype(BF16)
        for part in range(2):
            cache = chunk[(2 + part) * HEAD_SIZE : (3 + part) * HEAD_SIZE, :]
            found = dot_t(chooser, cache).astype(BF16)
            for rank in range(2):
                mine_ref[source, rank, part] = found[rank * PAGE_TOKENS : (rank + 1) * PAGE_TOKENS]
                other_ref[source, rank, part] = found[
                    (2 + rank) * PAGE_TOKENS : (3 + rank) * PAGE_TOKENS
                ]


def select_pages(chunks, offsets, after):
    out = shape((8, 2, 2, PAGE_TOKENS, HEAD_SIZE), BF16)
    return pl.pallas_call(
        functools.partial(pages_kernel, offsets),
        out_shape=(out, out),
        in_specs=[spec()] * len(chunks) + [spec(pl.ANY)],
        out_specs=(spec(), spec()),
        compiler_params=params(8),
        cost_estimate=SMALL,
        name="pages",
    )(*chunks, after)


def pool_kernel(mine_ref, came_ref, after_ref, out_ref):
    group = lax.axis_index("group")
    out_ref[:, group] = mine_ref[...]
    out_ref[:, 1 - group] = came_ref[...]


def pool(mine, came, after):
    return pl.pallas_call(
        pool_kernel,
        out_shape=shape((8, 2, 2, 2, PAGE_TOKENS, HEAD_SIZE), BF16),
        in_specs=[spec(), spec(), spec(pl.ANY)],
        out_specs=spec(),
        compiler_params=params(4),
        cost_estimate=SMALL,
        name="pool",
    )(mine, came, after)


def attend_rows(length_ref, query_ref, step_ref, cache_ref, attended_ref, score_ref, mixed_ref):
    count = HEADS * STEPS * ROWS
    query = jnp.concatenate(
        [
            query_ref[0, :, :, h * HEAD_SIZE : (h + 1) * HEAD_SIZE].reshape(STEPS * ROWS, HEAD_SIZE)
            for h in range(HEADS)
        ],
        axis=0,
    )
    scaling = HEAD_SIZE**-0.5

    def row_of(width):
        return lax.broadcasted_iota(jnp.int32, (count, width), 0) % ROWS

    row_wide, row_head = row_of(LEN), row_of(HEAD_SIZE)
    lengths = jnp.zeros((count, LEN), jnp.int32)
    for r in range(ROWS):
        score = dot_t(query, cache_ref[0, 0, r])
        if r == 0:
            score_ref[...] = score
        else:
            score_ref[...] = jnp.where(row_wide == r, score, score_ref[...])
        lengths = jnp.where(row_wide == r, length_ref[r], lengths)
    live = lax.broadcasted_iota(jnp.int32, (count, LEN), 1) < lengths
    score_old = jnp.where(live, score_ref[...] * scaling, LOW_SCORE)
    new_keys = step_ref[0, :, 0].reshape(STEPS * ROWS, HEAD_SIZE)
    new_values = step_ref[0, :, 1].reshape(STEPS * ROWS, HEAD_SIZE)
    lane = lax.broadcasted_iota(jnp.int32, (count, STEPS * ROWS), 1)
    place = lax.broadcasted_iota(jnp.int32, (count, STEPS * ROWS), 0)
    open_new = (lane % ROWS == place % ROWS) & (lane // ROWS <= place // ROWS % STEPS)
    score_new = jnp.where(open_new, dot_t(query, new_keys) * scaling, LOW_SCORE)
    top = jnp.maximum(
        jnp.max(score_old, axis=1, keepdims=True), jnp.max(score_new, axis=1, keepdims=True)
    )
    weight_old = jnp.where(live, jnp.exp(score_old - top), 0.0)
    weight_new = jnp.where(open_new, jnp.exp(score_new - top), 0.0)
    totals = jnp.sum(weight_old, axis=1, keepdims=True) + jnp.sum(weight_new, axis=1, keepdims=True)
    rounded = weight_old.astype(BF16)
    for r in range(ROWS):
        mixed = dot(rounded, cache_ref[0, 1, r])
        if r == 0:
            mixed_ref[...] = mixed
        else:
            mixed_ref[...] = jnp.where(row_head == r, mixed, mixed_ref[...])
    mixed = mixed_ref[...] + dot(weight_new.astype(BF16), new_values)
    attended = (mixed / totals).astype(BF16)
    for h in range(HEADS):
        attended_ref[:, h * HEAD_SIZE : (h + 1) * HEAD_SIZE] = attended[
            h * STEPS * ROWS : (h + 1) * STEPS * ROWS
        ]


TILES = 2


def decode_kernel(
    y_ref, length_ref, query_ref, step_ref, cache_ref, weight_ref, *refs
):
    outs, (attended_ref, score_ref, mixed_ref) = refs[:4], refs[4:]
    number = pl.program_id(0)

    @pl.when(number == 0)
    def _():
        attend_rows(length_ref, query_ref, step_ref, cache_ref, attended_ref, score_ref, mixed_ref)

    part = dot(attended_ref[...], weight_ref[...])
    for place, out in enumerate(outs):

        @pl.when(number // TILES == place)
        def _(out=out):
            out[...] = part.astype(out.dtype)


TURNS = (2, 1, 3, 0)


def decode(place, row_lengths, step_query, step_cache, row_cache, out_weight):
    width = QUARTER // TILES
    rows = STEPS * ROWS

    def weight_block(j, y):
        slot = j // TILES
        turn = jnp.where(slot == 0, 2, jnp.where(slot == 1, 1, jnp.where(slot == 2, 3, 0)))
        return (0, (y[0] + turn) % 4 * TILES + j % TILES)

    return pl.pallas_call(
        decode_kernel,
        out_shape=tuple(shape((rows, QUARTER), BF16 if t else F32) for t in TURNS),
        grid_spec=pltpu.PrefetchScalarGridSpec(
            num_scalar_prefetch=2,
            grid=(4 * TILES,),
            in_specs=[
                pl.BlockSpec(step_query.shape, lambda j, y, l: (0,) * 4),
                pl.BlockSpec(step_cache.shape, lambda j, y, l: (0,) * 5),
                pl.BlockSpec(row_cache.shape, lambda j, y, l: (0,) * 5),
                pl.BlockSpec((out_weight.shape[0], width), lambda j, y, l: weight_block(j, y)),
            ],
            out_specs=tuple(
                pl.BlockSpec(
                    (rows, width),
                    lambda j, y, l, s=s: (0, jnp.clip(j - s * TILES, 0, TILES - 1)),
                )
                for s in range(4)
            ),
            scratch_shapes=[
                pltpu.VMEM((rows, HEADS * HEAD_SIZE), BF16),
                pltpu.VMEM((HEADS * rows, LEN), F32),
                pltpu.VMEM((HEADS * rows, HEAD_SIZE), F32),
            ],
        ),
        compiler_params=params(56),
        cost_estimate=SMALL,
        name="decode",
    )(place, row_lengths, step_query, step_cache, row_cache, out_weight)


def quarter_kernel(own_ref, a_ref, b_ref, c_ref, after_ref, *outs):
    z = lax.axis_index("tp") % 4
    for out, turn in zip(outs, TURNS):
        columns = pl.ds(pl.multiple_of((z + turn) % 4 * SHARE, SHARE), SHARE)
        out[...] = (
            own_ref[:, columns]
            + a_ref[:, columns].astype(F32)
            + b_ref[:, columns].astype(F32)
            + c_ref[:, columns].astype(F32)
        )


def sum_quarters(own, came, after):
    return pl.pallas_call(
        quarter_kernel,
        out_shape=tuple(shape((STEPS * ROWS, SHARE), F32) for _ in TURNS),
        in_specs=[spec()] * 4 + [spec(pl.ANY)],
        out_specs=(spec(),) * 4,
        compiler_params=params(4),
        cost_estimate=SMALL,
        name="quarters",
    )(own, *came, after)


def diagonal():
    rows = lax.broadcasted_iota(jnp.int32, (STEPS * ROWS, HEAD_SIZE), 0)
    return rows == lax.broadcasted_iota(jnp.int32, (STEPS * ROWS, HEAD_SIZE), 1)


def hidden_kernel(residual_ref, own_ref, a_ref, b_ref, c_ref, after_ref, hidden_ref, square_ref):
    residual = residual_ref[0].reshape(STEPS * ROWS, SHARE).astype(F32)
    hidden = residual + (own_ref[...] + a_ref[...] + b_ref[...] + c_ref[...])
    hidden_ref[...] = hidden
    square = jnp.sum(hidden * hidden, axis=1, keepdims=True)
    square = jnp.sum(jnp.where(diagonal(), square, 0.0), axis=0, keepdims=True)
    square_ref[...] = jnp.broadcast_to(square[None], square_ref.shape)


def sum_shares(residual, own, came, after):
    return pl.pallas_call(
        hidden_kernel,
        out_shape=(
            shape((STEPS * ROWS, SHARE), F32),
            shape((16, 8, HEAD_SIZE), F32),
        ),
        in_specs=[spec()] * 5 + [spec(pl.ANY)],
        out_specs=(spec(), spec()),
        compiler_params=params(4),
        cost_estimate=SMALL,
        name="hidden",
    )(residual, own, *came, after)


def finish_kernel(hidden_ref, gain_ref, square_ref, after_ref, out_ref):
    square = jnp.sum(square_ref[...], axis=0)[0:1]
    square = jnp.sum(jnp.where(diagonal(), square, 0.0), axis=1, keepdims=True)
    scale = lax.rsqrt(square * (1.0 / COLUMNS) + EPSILON)
    out = hidden_ref[...] * scale * gain_ref[...].reshape(1, SHARE).astype(F32)
    out_ref[0] = out.astype(BF16).reshape(STEPS, ROWS, SHARE)


def finish(hidden, gain, squares, after):
    return pl.pallas_call(
        finish_kernel,
        out_shape=shape((1, STEPS, ROWS, SHARE), BF16),
        in_specs=[spec()] * 3 + [spec(pl.ANY)],
        out_specs=spec(),
        compiler_params=params(4),
        cost_estimate=SMALL,
        name="finish",
    )(hidden, gain, squares, after)


def move_x(a, turn):
    return lax.ppermute(a, "blk", [(i, i // 4 * 4 + (i + turn) % 4) for i in range(8)])


def move_y(a, turn):
    return lax.ppermute(a, "tp", [(i, (i + 4 * turn) % 16) for i in range(16)])


def move_z(a, turn):
    return lax.ppermute(a, "tp", [(i, i // 4 * 4 + (i + turn) % 4) for i in range(16)])


def body(
    prompt_query,
    context_cache,
    new_block_cache,
    block_offset,
    page_owner,
    step_query,
    step_cache,
    row_cache,
    row_lengths,
    out_weight,
    residual,
    norm_gain,
):
    packed = pack(
        page_owner.reshape(PAGES),
        jnp.swapaxes(context_cache, 2, 3),
        jnp.swapaxes(new_block_cache, 2, 3),
    )
    near = lax.ppermute(packed, "tp", [(i, i ^ 1) for i in range(16)])
    far = lax.ppermute(packed, "blk", [(i, i ^ 4) for i in range(8)])
    far_near = lax.ppermute(
        packed,
        ("blk", "tp"),
        [(b * 16 + t, (b ^ 4) * 16 + (t ^ 1)) for b in range(8) for t in range(16)],
    )
    place = (lax.axis_index("tp") // 4).astype(jnp.int32).reshape(1)
    parts = decode(
        place, row_lengths.reshape(ROWS), step_query, step_cache, row_cache, out_weight
    )
    came = [move_y(a, turn) for a, turn in zip(parts[:3], TURNS)]

    chunk = join(packed, near, parts[3])
    up = move_x(chunk, 1)
    down = move_x(chunk, 3)
    chunk_far = join(far, far_near, chunk)
    far_up = move_x(chunk_far, 1)
    far_down = move_x(chunk_far, 3)
    up_two = move_x(up, 1)
    far_down_two = move_x(far_down, 3)

    state = attend(
        block_offset, prompt_query, [chunk, chunk_far], [(0, 0), (1, 0)], None, False, chunk_far
    )
    shares = sum_quarters(parts[3], came, state[0])
    came = [move_z(a, turn) for a, turn in zip(shares[:3], TURNS)]
    state = attend(
        block_offset,
        prompt_query,
        [up, down, far_up, far_down],
        [(0, -1), (0, 1), (1, -1), (1, 1)],
        state,
        False,
        shares[3],
    )
    hidden, square = sum_shares(residual, shares[3], came, state[0])
    squares = lax.all_to_all(square, "tp", split_axis=0, concat_axis=0, tiled=True)
    chunks = [chunk, chunk_far, up, down, far_up, far_down, up_two, far_down_two]
    offsets = [(0, 0), (1, 0), (0, -1), (0, 1), (1, -1), (1, 1), (0, 2), (1, 2)]
    mine, other = select_pages(chunks, offsets, hidden)
    other = lax.ppermute(other, "group", [(0, 1), (1, 0)])
    prefill_out = attend(
        block_offset, prompt_query, [up_two, far_down_two], [(0, 2), (1, 2)], state, True, mine
    )
    page_pool = pool(mine, other, prefill_out).reshape(1, 32, 2, PAGE_TOKENS, HEAD_SIZE)
    decode_out = finish(hidden, norm_gain, squares, page_pool)
    return (prefill_out, page_pool, decode_out)


def solution(mesh):
    placed = (
        P("group", "blk", "tp"),
        P("group", None, "blk", "tp"),
        P("group", None, "blk", "tp"),
        P(),
        P("group", "blk", None),
        P(("blk", "group"), None, None, "tp"),
        P(("blk", "group"), None, None, None, "tp"),
        P(("blk", "group"), None, None, None, "tp"),
        P(("blk", "group"), None),
        P("tp", None),
        P(("blk", "group"), None, None, "tp"),
        P("tp"),
    )
    return jax.shard_map(
        body,
        mesh=mesh,
        in_specs=placed,
        out_specs=(
            P("group", "blk", "tp"),
            P(("blk", "group"), None, None, None, "tp"),
            P(("blk", "group"), None, None, "tp"),
        ),
        check_vma=False,
    )
```

```python
import functools
import math

import jax
import jax.numpy as jnp
from jax import lax
from jax.experimental import pallas as pl
from jax.experimental.pallas import tpu as pltpu
from jax.sharding import PartitionSpec as P

HEAD_SIZE = 128
PAGE_TOKENS = 16
STEPS = 4
ROWS = 16
LEN = 256
HEADS = 4
TOKENS = 256
PAGES = TOKENS // PAGE_TOKENS
HALF = HEAD_SIZE // 2
PACKED = 4 * HALF
CHUNK = 4 * HEAD_SIZE
TAIL = 16
PIECE = CHUNK + TAIL
COLUMNS = 8192
QUARTER = COLUMNS // 4
SHARE = COLUMNS // 16
LOW_SCORE = -1e30
EPSILON = 1e-05
F32 = jnp.float32
BF16 = jnp.bfloat16
LOG2_SCALE = math.log2(math.e) * HEAD_SIZE**-0.5
VMEM = pltpu.VMEM
SMEM = pltpu.SMEM
MIB = 1024 * 1024
WHOLE = 60.5


def params(mebibytes):
    return pltpu.CompilerParams(vmem_limit_bytes=int(mebibytes * MIB))


def spec(space=VMEM):
    return pl.BlockSpec(memory_space=space)


def shape(dims, dtype):
    return jax.ShapeDtypeStruct(dims, dtype)


def dot_t(a, b):
    return lax.dot_general(a, b, (((1,), (1,)), ((), ())), preferred_element_type=F32)


def dot(a, b):
    return lax.dot_general(a, b, (((1,), (0,)), ((), ())), preferred_element_type=F32)


TOKEN = shape((8, HEAD_SIZE), F32)


def run(kernel, title, mebibytes, token, outs, operands, scratch=(), emit=True, cost=0):
    tokens = [] if token is None else [token]
    count = len(operands) + len(tokens)

    def with_token(*refs):
        results, rest = refs[count : count + len(outs)], refs[count + len(outs) :]
        if emit:
            gone, *rest = rest
            gone[...] = refs[len(operands)][...] if tokens else jnp.zeros(gone.shape, gone.dtype)
        kernel(*refs[: len(operands)], *results, *rest)

    return pl.pallas_call(
        with_token,
        out_shape=(*outs, TOKEN) if emit else tuple(outs),
        in_specs=[spec(space) for _, space in operands] + [spec()] * len(tokens),
        out_specs=(spec(),) * (len(outs) + emit),
        scratch_shapes=list(scratch),
        compiler_params=params(mebibytes),
        cost_estimate=pl.CostEstimate(
            flops=1024 + 1150000000 * cost, bytes_accessed=1024, transcendentals=0
        ),
        name=title,
    )(*[a for a, _ in operands], *tokens)


def pack_kernel(owner_hbm, context_hbm, block_hbm, out_ref, owner_ref, sems):
    copies = [pltpu.make_async_copy(owner_hbm, owner_ref, sems.at[4])]
    for number in range(4):
        source = context_hbm if number < 2 else block_hbm
        copies.append(
            pltpu.make_async_copy(
                source.at[0, number % 2],
                out_ref.at[pl.ds(number * HALF, HALF), :],
                sems.at[number],
            )
        )
    for copy in copies:
        copy.start()
    copies[0].wait()
    owners = [owner_ref[0, p] for p in range(PAGES)]
    page = lax.broadcasted_iota(jnp.int32, (TAIL, TOKENS), 1) // PAGE_TOKENS
    codes = jnp.full((TAIL, TOKENS), -1, jnp.int32)
    for p in range(PAGES):
        rank = jnp.int32(0)
        for q in range(p):
            rank = rank + (owners[q] == owners[p]).astype(jnp.int32)
        codes = jnp.where(page == p, owners[p] * 2 + rank, codes)
    out_ref[PACKED:, :] = codes.astype(F32).astype(BF16)
    for copy in copies[1:]:
        copy.wait()


def pack(page_owner, context_cache, new_block_cache):
    return run(
        pack_kernel,
        "pack",
        WHOLE,
        None,
        [shape((PACKED + TAIL, TOKENS), BF16)],
        [(a, pl.ANY) for a in (page_owner, context_cache, new_block_cache)],
        [pltpu.SMEM((1, PAGES), jnp.int32), pltpu.SemaphoreType.DMA((5,))],
        emit=False,
    )[0]


def join_kernel(mine_ref, near_ref, far_ref, far_near_ref, out_ref):
    odd = lax.axis_index("tp") % 2
    for base, first_ref, second_ref in ((0, mine_ref, near_ref), (PIECE, far_ref, far_near_ref)):
        for number in range(4):
            rows = slice(number * HALF, (number + 1) * HALF)
            here = pl.multiple_of(base + number * HEAD_SIZE + odd * HALF, 16)
            there = pl.multiple_of(base + number * HEAD_SIZE + (1 - odd) * HALF, 16)
            out_ref[pl.ds(here, HALF), :] = first_ref[rows, :]
            out_ref[pl.ds(there, HALF), :] = second_ref[rows, :]
        out_ref[base + CHUNK : base + PIECE, :] = first_ref[PACKED:, :]


def join(mine, near, far, far_near, token):
    outs = [shape((2 * PIECE, TOKENS), BF16)]
    operands = [(a, VMEM) for a in (mine, near, far, far_near)]
    return run(join_kernel, "join", 4, token, outs, operands)


def relay_kernel(up_ref, down_ref, up_out, down_out):
    up_out[...] = up_ref[:PIECE, :]
    down_out[...] = down_ref[PIECE:, :]


def relay(up, down, token):
    outs = [shape((PIECE, TOKENS), BF16)] * 2
    operands = [(up, VMEM), (down, VMEM)]
    return run(relay_kernel, "relay", 4, token, outs, operands, cost=2)


def source_of(flip, turn):
    blk = lax.axis_index("blk")
    return (blk // 4 + flip) % 2 * 4 + (blk % 4 + turn + 4) % 4


def attend_kernel(places, first, last, early, *refs):
    offset_ref, query_ref = refs[:2]
    arrays = 1 + max(place[0] for place in places)
    chunks = refs[2 : 2 + arrays]
    refs = refs[2 + arrays :]
    if not first:
        top_in, sum_in = refs[:2]
        refs = refs[2:]
    refs = refs[early:]
    blk = lax.axis_index("blk")
    offset = offset_ref[lax.axis_index("group")]
    key_number = lax.broadcasted_iota(jnp.int32, (TOKENS, TOKENS), 0)
    query_number = lax.broadcasted_iota(jnp.int32, (TOKENS, TOKENS), 1)
    queries = [
        query_ref[0, :, h * HEAD_SIZE : (h + 1) * HEAD_SIZE].T for h in range(HEADS)
    ]
    ones = jnp.ones((TAIL, TOKENS), BF16)
    groups = []
    for number, base, flip, turn in places:
        source = source_of(flip, turn)
        parts = [
            chunks[number][base + n * HEAD_SIZE : base + (n + 1) * HEAD_SIZE, :] for n in range(4)
        ]
        open_context = jnp.where(source * TOKENS + key_number < offset, 0.0, LOW_SCORE)
        open_block = jnp.where(source <= blk, 0.0, LOW_SCORE)
        groups.append(
            [
                (parts[0].T, jnp.concatenate([parts[1], ones], axis=0), open_context, False),
                (
                    parts[2].T,
                    jnp.concatenate([parts[3], ones], axis=0),
                    open_block,
                    (flip, turn) == (0, 0),
                ),
            ]
        )

    def scores_of(group, head):
        scores = []
        for key, _, bias, diagonal in group:
            score = dot(key, queries[head]) * LOG2_SCALE + bias
            if diagonal:
                score = jnp.where(key_number <= query_number, score, LOW_SCORE)
            scores.append(score)
        return scores

    steps = [(group, head) for group in groups for head in range(HEADS)]
    tops = [jnp.full((1, TOKENS), LOW_SCORE, F32) if first else top_in[h, 0:1] for h in range(HEADS)]
    sums = [None if first else sum_in[h] for h in range(HEADS)]
    ahead = scores_of(*steps[0])
    for number, (group, head) in enumerate(steps):
        scores = ahead
        if number + 1 < len(steps):
            ahead = scores_of(*steps[number + 1])
        top = jnp.maximum(
            tops[head], jnp.max(jnp.maximum(scores[0], scores[1]), axis=0, keepdims=True)
        )
        fresh = None
        for score, (_, value, _, _) in zip(scores, group):
            weight = jnp.exp2(score - top)
            high = weight.astype(BF16)
            low = (weight - high.astype(F32)).astype(BF16)
            part = dot(value, high) + dot(value, low)
            fresh = part if fresh is None else fresh + part
        if sums[head] is not None:
            fresh = sums[head] * jnp.exp2(tops[head] - top) + fresh
        sums[head] = fresh
        tops[head] = top
    for head in range(HEADS):
        if last:
            (out_ref,) = refs
            mixed = sums[head][:HEAD_SIZE] / sums[head][HEAD_SIZE : HEAD_SIZE + 1]
            out_ref[0, :, head * HEAD_SIZE : (head + 1) * HEAD_SIZE] = mixed.T.astype(BF16)
        else:
            top_out, sum_out = refs
            top_out[head] = jnp.broadcast_to(tops[head], (8, TOKENS))
            sum_out[head] = sums[head]


def attend(block_offset, queries, chunks, places, state, last, token, early=()):
    first = state is None
    if last:
        outs = [shape((1, TOKENS, HEADS * HEAD_SIZE), BF16)]
    else:
        outs = [
            shape((HEADS, 8, TOKENS), F32),
            shape((HEADS, HEAD_SIZE + TAIL, TOKENS), F32),
        ]
    operands = [(block_offset, SMEM)]
    operands += [(a, VMEM) for a in (queries, *chunks, *(() if first else state), *early)]
    return run(
        functools.partial(attend_kernel, places, first, last, len(early)),
        "attend",
        24,
        token,
        outs,
        operands,
        cost=3,
    )


def pages_kernel(places, *refs):
    chunks, (mine_ref, other_ref) = refs[:-2], refs[-2:]
    instance = lax.axis_index("blk") * 2 + lax.axis_index("group")
    other = lax.axis_index("blk") * 2 + 1 - lax.axis_index("group")
    slots = 4 * PAGE_TOKENS
    row = lax.broadcasted_iota(jnp.int32, (slots, TOKENS), 0)
    lane = lax.broadcasted_iota(jnp.int32, (slots, TOKENS), 1)
    wanted = jnp.where(row < 2 * PAGE_TOKENS, instance * 2, other * 2) + row // PAGE_TOKENS % 2
    wanted = jnp.where(row % PAGE_TOKENS == lane % PAGE_TOKENS, wanted, -2).astype(F32)
    for number, base, flip, turn in places:
        source = source_of(flip, turn)
        chunk = chunks[number]
        codes = chunk[base + CHUNK : base + PIECE, :].astype(F32)[0:1]
        chooser = jnp.where(wanted == codes, 1.0, 0.0).astype(BF16)
        for part in range(2):
            start = base + (2 + part) * HEAD_SIZE
            found = dot_t(chooser, chunk[start : start + HEAD_SIZE, :]).astype(BF16)
            for rank in range(2):
                mine_ref[source, rank, part] = found[rank * PAGE_TOKENS : (rank + 1) * PAGE_TOKENS]
                other_ref[source, rank, part] = found[
                    (2 + rank) * PAGE_TOKENS : (3 + rank) * PAGE_TOKENS
                ]


def select_pages(chunks, places, token):
    out = shape((8, 2, 2, PAGE_TOKENS, HEAD_SIZE), BF16)
    return run(
        functools.partial(pages_kernel, places),
        "pages",
        8,
        token,
        [out, out],
        [(a, VMEM) for a in chunks],
    )


def pool_kernel(mine_ref, came_ref, out_ref):
    group = lax.axis_index("group")
    out_ref[:, group] = mine_ref[...]
    out_ref[:, 1 - group] = came_ref[...]


def pool(mine, came, token):
    out = shape((8, 2, 2, 2, PAGE_TOKENS, HEAD_SIZE), BF16)
    return run(pool_kernel, "pool", 4, token, [out], [(mine, VMEM), (came, VMEM)])


def attend_rows(
    length_ref, query_ref, step_ref, cache_ref, attended_ref, score_ref, mixed_ref, waits
):
    count = HEADS * STEPS * ROWS
    query = jnp.concatenate(
        [
            query_ref[0, :, :, h * HEAD_SIZE : (h + 1) * HEAD_SIZE].reshape(STEPS * ROWS, HEAD_SIZE)
            for h in range(HEADS)
        ],
        axis=0,
    )
    scaling = HEAD_SIZE**-0.5

    def row_of(width):
        return lax.broadcasted_iota(jnp.int32, (count, width), 0) % ROWS

    row_wide, row_head = row_of(LEN), row_of(HEAD_SIZE)
    lengths = jnp.zeros((count, LEN), jnp.int32)
    for r in range(ROWS):
        if r % (ROWS // 2) == 0:
            waits[r // (ROWS // 2)].wait()
        score = dot_t(query, cache_ref[0, 0, r])
        if r == 0:
            score_ref[...] = score
        else:
            score_ref[...] = jnp.where(row_wide == r, score, score_ref[...])
        lengths = jnp.where(row_wide == r, length_ref[0, r], lengths)
    live = lax.broadcasted_iota(jnp.int32, (count, LEN), 1) < lengths
    score_old = jnp.where(live, score_ref[...] * scaling, LOW_SCORE)
    new_keys = step_ref[0, :, 0].reshape(STEPS * ROWS, HEAD_SIZE)
    new_values = step_ref[0, :, 1].reshape(STEPS * ROWS, HEAD_SIZE)
    lane = lax.broadcasted_iota(jnp.int32, (count, STEPS * ROWS), 1)
    place = lax.broadcasted_iota(jnp.int32, (count, STEPS * ROWS), 0)
    open_new = (lane % ROWS == place % ROWS) & (lane // ROWS <= place // ROWS % STEPS)
    score_new = jnp.where(open_new, dot_t(query, new_keys) * scaling, LOW_SCORE)
    top = jnp.maximum(
        jnp.max(score_old, axis=1, keepdims=True), jnp.max(score_new, axis=1, keepdims=True)
    )
    weight_old = jnp.where(live, jnp.exp(score_old - top), 0.0)
    weight_new = jnp.where(open_new, jnp.exp(score_new - top), 0.0)
    totals = jnp.sum(weight_old, axis=1, keepdims=True) + jnp.sum(weight_new, axis=1, keepdims=True)
    rounded = weight_old.astype(BF16)
    for r in range(ROWS):
        if r % (ROWS // 2) == 0:
            waits[2 + r // (ROWS // 2)].wait()
        mixed = dot(rounded, cache_ref[0, 1, r])
        if r == 0:
            mixed_ref[...] = mixed
        else:
            mixed_ref[...] = jnp.where(row_head == r, mixed, mixed_ref[...])
    mixed = mixed_ref[...] + dot(weight_new.astype(BF16), new_values)
    attended = (mixed / totals).astype(BF16)
    for h in range(HEADS):
        attended_ref[:, h * HEAD_SIZE : (h + 1) * HEAD_SIZE] = attended[
            h * STEPS * ROWS : (h + 1) * STEPS * ROWS
        ]


TURNS = (2, 1, 3, 0)
SPLIT = 2
WIDTH = QUARTER // SPLIT


def decode_kernel(length_hbm, query_hbm, step_hbm, cache_hbm, weight_hbm, *refs):
    outs = refs[:4]
    length_ref, query_ref, step_ref, cache_ref, weight_ref = refs[4:9]
    attended_ref, score_ref, mixed_ref, row_sems, cache_sems, weight_sems = refs[9:]
    firsts = [
        pltpu.make_async_copy(query_hbm, query_ref, row_sems.at[0]),
        pltpu.make_async_copy(step_hbm, step_ref, row_sems.at[1]),
        pltpu.make_async_copy(length_hbm, length_ref, row_sems.at[2]),
    ]
    waits = []
    for number in range(4):
        rows = pl.ds(number % 2 * (ROWS // 2), ROWS // 2)
        waits.append(
            pltpu.make_async_copy(
                cache_hbm.at[0, number // 2, rows],
                cache_ref.at[0, number // 2, rows],
                cache_sems.at[number],
            )
        )
    y = lax.axis_index("tp") // 4
    copies = []
    for number in range(4 * SPLIT):
        column = (y + TURNS[number // SPLIT]) % 4 * QUARTER + number % SPLIT * WIDTH
        copies.append(
            pltpu.make_async_copy(
                weight_hbm.at[:, pl.ds(pl.multiple_of(column, WIDTH), WIDTH)],
                weight_ref.at[number],
                weight_sems.at[number],
            )
        )
    for copy in firsts + waits + copies:
        copy.start()
    for copy in firsts:
        copy.wait()
    attend_rows(
        length_ref, query_ref, step_ref, cache_ref, attended_ref, score_ref, mixed_ref, waits
    )
    attended = attended_ref[...]
    for number, copy in enumerate(copies):
        copy.wait()
        part = dot(attended, weight_ref[number])
        out = outs[number // SPLIT]
        columns = slice(number % SPLIT * WIDTH, (number % SPLIT + 1) * WIDTH)
        out[:, columns] = part.astype(out.dtype)


def decode(row_lengths, step_query, step_cache, row_cache, out_weight):
    rows = STEPS * ROWS
    operands = (row_lengths, step_query, step_cache, row_cache, out_weight)
    return run(
        decode_kernel,
        "decode",
        WHOLE - 1.95,
        None,
        [shape((rows, QUARTER), BF16 if turn else F32) for turn in TURNS],
        [(a, pl.ANY) for a in operands],
        [
            pltpu.SMEM((1, ROWS), jnp.int32),
            pltpu.VMEM(step_query.shape, BF16),
            pltpu.VMEM(step_cache.shape, BF16),
            pltpu.VMEM(row_cache.shape, BF16),
            pltpu.VMEM((4 * SPLIT, out_weight.shape[0], WIDTH), BF16),
            pltpu.VMEM((rows, HEADS * HEAD_SIZE), BF16),
            pltpu.VMEM((HEADS * rows, LEN), F32),
            pltpu.VMEM((HEADS * rows, HEAD_SIZE), F32),
            pltpu.SemaphoreType.DMA((3,)),
            pltpu.SemaphoreType.DMA((4,)),
            pltpu.SemaphoreType.DMA((4 * SPLIT,)),
        ],
        cost=9,
    )


def quarter_kernel(own_ref, a_ref, b_ref, c_ref, *outs):
    z = lax.axis_index("tp") % 4
    for out, turn in zip(outs, TURNS):
        columns = pl.ds(pl.multiple_of((z + turn) % 4 * SHARE, SHARE), SHARE)
        out[...] = (
            own_ref[:, columns]
            + a_ref[:, columns].astype(F32)
            + b_ref[:, columns].astype(F32)
            + c_ref[:, columns].astype(F32)
        )


def sum_quarters(own, came, token):
    outs = [shape((STEPS * ROWS, SHARE), F32) for _ in TURNS]
    operands = [(a, VMEM) for a in (own, *came)]
    return run(quarter_kernel, "quarters", 4, token, outs, operands, cost=4)


def diagonal():
    rows = lax.broadcasted_iota(jnp.int32, (STEPS * ROWS, HEAD_SIZE), 0)
    return rows == lax.broadcasted_iota(jnp.int32, (STEPS * ROWS, HEAD_SIZE), 1)


def hidden_kernel(residual_ref, own_ref, a_ref, b_ref, c_ref, hidden_ref, square_ref):
    residual = residual_ref[0].reshape(STEPS * ROWS, SHARE).astype(F32)
    hidden = residual + (own_ref[...] + a_ref[...] + b_ref[...] + c_ref[...])
    hidden_ref[...] = hidden
    square = jnp.sum(hidden * hidden, axis=1, keepdims=True)
    square = jnp.sum(jnp.where(diagonal(), square, 0.0), axis=0, keepdims=True)
    square_ref[...] = jnp.broadcast_to(square[None], square_ref.shape)


def sum_shares(residual, own, came, token):
    outs = [shape((STEPS * ROWS, SHARE), F32), shape((16, 8, HEAD_SIZE), F32)]
    operands = [(a, VMEM) for a in (residual, own, *came)]
    return run(hidden_kernel, "hidden", 4, token, outs, operands)


def finish_kernel(hidden_ref, gain_ref, square_ref, out_ref):
    square = jnp.sum(square_ref[...], axis=0)[0:1]
    square = jnp.sum(jnp.where(diagonal(), square, 0.0), axis=1, keepdims=True)
    scale = lax.rsqrt(square * (1.0 / COLUMNS) + EPSILON)
    out = hidden_ref[...] * scale * gain_ref[...].reshape(1, SHARE).astype(F32)
    out_ref[0] = out.astype(BF16).reshape(STEPS, ROWS, SHARE)


def finish(hidden, gain, squares, token):
    outs = [shape((1, STEPS, ROWS, SHARE), BF16)]
    operands = [(a, VMEM) for a in (hidden, gain, squares)]
    return run(finish_kernel, "finish", 4, token, outs, operands)


def move_x(a, turn):
    return lax.ppermute(a, "blk", [(i, i // 4 * 4 + (i + turn) % 4) for i in range(8)])


def move_y(a, turn):
    return lax.ppermute(a, "tp", [(i, (i + 4 * turn) % 16) for i in range(16)])


def move_z(a, turn):
    return lax.ppermute(a, "tp", [(i, i // 4 * 4 + (i + turn) % 4) for i in range(16)])


def body(
    prompt_query,
    context_cache,
    new_block_cache,
    block_offset,
    page_owner,
    step_query,
    step_cache,
    row_cache,
    row_lengths,
    out_weight,
    residual,
    norm_gain,
):
    packed = pack(
        page_owner.reshape(1, PAGES),
        jnp.swapaxes(context_cache, 2, 3),
        jnp.swapaxes(new_block_cache, 2, 3),
    )
    near = lax.ppermute(packed, "tp", [(i, i ^ 1) for i in range(16)])
    far = lax.ppermute(packed, "blk", [(i, i ^ 4) for i in range(8)])
    far_near = lax.ppermute(
        packed,
        ("blk", "tp"),
        [(b * 16 + t, (b ^ 4) * 16 + (t ^ 1)) for b in range(8) for t in range(16)],
    )
    *parts, own, token = decode(row_lengths, step_query, step_cache, row_cache, out_weight)
    came = [move_y(a, turn) for a, turn in zip(parts, TURNS)]
    here, token = join(packed, near, far, far_near, token)
    up = move_x(here, 1)
    down = move_x(here, 3)
    *state, token = attend(
        block_offset,
        prompt_query,
        [here],
        [(0, 0, 0, 0), (0, PIECE, 1, 0)],
        None,
        False,
        token,
        [own],
    )
    *shares, own, token = sum_quarters(own, came, token)
    came = [move_z(a, turn) for a, turn in zip(shares, TURNS)]
    up_two, down_two, token = relay(up, down, token)
    up_two = move_x(up_two, 1)
    down_two = move_x(down_two, 3)
    places = [(0, 0, 0, -1), (0, PIECE, 1, -1), (1, 0, 0, 1), (1, PIECE, 1, 1)]
    *state, token = attend(block_offset, prompt_query, [up, down], places, state, False, token)
    hidden, square, token = sum_shares(residual, own, came, token)
    squares = lax.all_to_all(square, "tp", split_axis=0, concat_axis=0, tiled=True)
    places = [(0, 0, 0, 0), (0, PIECE, 1, 0), (1, 0, 0, -1), (1, PIECE, 1, -1)]
    places += [(2, 0, 0, 1), (2, PIECE, 1, 1), (3, 0, 0, 2), (4, 0, 1, 2)]
    mine, other, token = select_pages([here, up, down, up_two, down_two], places, token)
    other = lax.ppermute(other, "group", [(0, 1), (1, 0)])
    prefill_out, token = attend(
        block_offset,
        prompt_query,
        [up_two, down_two],
        [(0, 0, 0, 2), (1, 0, 1, 2)],
        state,
        True,
        token,
    )
    page_pool, token = pool(mine, other, token)
    decode_out, token = finish(hidden, norm_gain, squares, token)
    return (prefill_out, page_pool.reshape(1, 32, 2, PAGE_TOKENS, HEAD_SIZE), decode_out)


def solution(mesh):
    placed = (
        P("group", "blk", "tp"),
        P("group", None, "blk", "tp"),
        P("group", None, "blk", "tp"),
        P(),
        P("group", "blk", None),
        P(("blk", "group"), None, None, "tp"),
        P(("blk", "group"), None, None, None, "tp"),
        P(("blk", "group"), None, None, None, "tp"),
        P(("blk", "group"), None),
        P("tp", None),
        P(("blk", "group"), None, None, "tp"),
        P("tp"),
    )
    return jax.shard_map(
        body,
        mesh=mesh,
        in_specs=placed,
        out_specs=(
            P("group", "blk", "tp"),
            P(("blk", "group"), None, None, None, "tp"),
            P(("blk", "group"), None, None, "tp"),
        ),
        check_vma=False,
    )
```

```python
import functools
import math

import jax
import jax.numpy as jnp
from jax import lax
from jax.experimental import pallas as pl
from jax.experimental.pallas import tpu as pltpu
from jax.sharding import PartitionSpec as P

HEAD_SIZE = 128
PAGE_TOKENS = 16
STEPS = 4
ROWS = 16
LEN = 256
HEADS = 4
TOKENS = 256
PAGES = TOKENS // PAGE_TOKENS
HALF = HEAD_SIZE // 2
PACKED = 4 * HALF
CHUNK = 4 * HEAD_SIZE
TAIL = 16
PIECE = CHUNK + TAIL
COLUMNS = 8192
QUARTER = COLUMNS // 4
SHARE = COLUMNS // 16
LOW_SCORE = -1e30
EPSILON = 1e-05
F32 = jnp.float32
BF16 = jnp.bfloat16
LOG2_SCALE = math.log2(math.e) * HEAD_SIZE**-0.5
VMEM = pltpu.VMEM
SMEM = pltpu.SMEM
MIB = 1024 * 1024
WHOLE = 60


def params(mebibytes):
    return pltpu.CompilerParams(vmem_limit_bytes=int(mebibytes * MIB))


def spec(space=VMEM):
    return pl.BlockSpec(memory_space=space)


def shape(dims, dtype):
    return jax.ShapeDtypeStruct(dims, dtype)


def dot_t(a, b):
    return lax.dot_general(a, b, (((1,), (1,)), ((), ())), preferred_element_type=F32)


def dot(a, b):
    return lax.dot_general(a, b, (((1,), (0,)), ((), ())), preferred_element_type=F32)


TOKEN = shape((8, HEAD_SIZE), F32)


def run(kernel, title, mebibytes, token, outs, operands, scratch=(), emit=True, cost=0):
    tokens = [] if token is None else [token]
    count = len(operands) + len(tokens)

    def with_token(*refs):
        results, rest = refs[count : count + len(outs)], refs[count + len(outs) :]
        if emit:
            gone, *rest = rest
            gone[...] = refs[len(operands)][...] if tokens else jnp.zeros(gone.shape, gone.dtype)
        kernel(*refs[: len(operands)], *results, *rest)

    return pl.pallas_call(
        with_token,
        out_shape=(*outs, TOKEN) if emit else tuple(outs),
        in_specs=[spec(space) for _, space in operands] + [spec()] * len(tokens),
        out_specs=(spec(),) * (len(outs) + emit),
        scratch_shapes=list(scratch),
        compiler_params=params(mebibytes),
        cost_estimate=pl.CostEstimate(
            flops=1024 + 1150000000 * cost, bytes_accessed=1024, transcendentals=0
        ),
        name=title,
    )(*[a for a, _ in operands], *tokens)


def pack_kernel(owner_hbm, context_hbm, block_hbm, out_ref, owner_ref, sems):
    copies = [pltpu.make_async_copy(owner_hbm, owner_ref, sems.at[4])]
    for number in range(4):
        source = context_hbm if number < 2 else block_hbm
        copies.append(
            pltpu.make_async_copy(
                source.at[0, number % 2],
                out_ref.at[pl.ds(number * HALF, HALF), :],
                sems.at[number],
            )
        )
    for copy in copies:
        copy.start()
    copies[0].wait()
    owners = [owner_ref[0, p] for p in range(PAGES)]
    page = lax.broadcasted_iota(jnp.int32, (TAIL, TOKENS), 1) // PAGE_TOKENS
    codes = jnp.full((TAIL, TOKENS), -1, jnp.int32)
    for p in range(PAGES):
        rank = jnp.int32(0)
        for q in range(p):
            rank = rank + (owners[q] == owners[p]).astype(jnp.int32)
        codes = jnp.where(page == p, owners[p] * 2 + rank, codes)
    out_ref[PACKED:, :] = codes.astype(F32).astype(BF16)
    for copy in copies[1:]:
        copy.wait()


def pack(page_owner, context_cache, new_block_cache):
    return run(
        pack_kernel,
        "pack",
        WHOLE,
        None,
        [shape((PACKED + TAIL, TOKENS), BF16)],
        [(a, pl.ANY) for a in (page_owner, context_cache, new_block_cache)],
        [pltpu.SMEM((1, PAGES), jnp.int32), pltpu.SemaphoreType.DMA((5,))],
        emit=False,
    )[0]


def join_kernel(mine_ref, near_ref, far_ref, far_near_ref, out_ref):
    odd = lax.axis_index("tp") % 2
    for base, first_ref, second_ref in ((0, mine_ref, near_ref), (PIECE, far_ref, far_near_ref)):
        for number in range(4):
            rows = slice(number * HALF, (number + 1) * HALF)
            here = pl.multiple_of(base + number * HEAD_SIZE + odd * HALF, 16)
            there = pl.multiple_of(base + number * HEAD_SIZE + (1 - odd) * HALF, 16)
            out_ref[pl.ds(here, HALF), :] = first_ref[rows, :]
            out_ref[pl.ds(there, HALF), :] = second_ref[rows, :]
        out_ref[base + CHUNK : base + PIECE, :] = first_ref[PACKED:, :]


def join(mine, near, far, far_near, token):
    outs = [shape((2 * PIECE, TOKENS), BF16)]
    operands = [(a, VMEM) for a in (mine, near, far, far_near)]
    return run(join_kernel, "join", 4, token, outs, operands)


def relay_kernel(up_ref, down_ref, up_out, down_out):
    up_out[...] = up_ref[:PIECE, :]
    down_out[...] = down_ref[PIECE:, :]


def relay(up, down, token):
    outs = [shape((PIECE, TOKENS), BF16)] * 2
    operands = [(up, VMEM), (down, VMEM)]
    return run(relay_kernel, "relay", 4, token, outs, operands, cost=2)


def source_of(flip, turn):
    blk = lax.axis_index("blk")
    return (blk // 4 + flip) % 2 * 4 + (blk % 4 + turn + 4) % 4


def attend_kernel(places, first, last, early, *refs):
    offset_ref, query_ref = refs[:2]
    arrays = 1 + max(place[0] for place in places)
    chunks = refs[2 : 2 + arrays]
    refs = refs[2 + arrays :]
    start = None
    if not first:
        start = refs[:2]
        refs = refs[2:]
    refs = refs[early:]
    if last:
        out_ref, *refs = refs
    top_ref, sum_ref = refs
    blk = lax.axis_index("blk")
    offset = offset_ref[lax.axis_index("group")]
    key_number = lax.broadcasted_iota(jnp.int32, (TOKENS, TOKENS), 0)
    query_number = lax.broadcasted_iota(jnp.int32, (TOKENS, TOKENS), 1)
    queries = [query_ref[0, :, h * HEAD_SIZE : (h + 1) * HEAD_SIZE].T for h in range(HEADS)]
    ones = jnp.ones((TAIL, TOKENS), BF16)

    def context_tile(number, base, flip, turn):
        start = source_of(flip, turn) * TOKENS
        bias = jnp.where(start + key_number < offset, 0.0, LOW_SCORE)
        return (number, base, lambda score: score + bias)

    def diagonal_tile(number, base):
        low = jnp.where(key_number <= query_number, 0.0, LOW_SCORE)
        return (number, base + 2 * HEAD_SIZE, lambda score: score + low)

    def masked_tile(number, base, flip, turn):
        low = jnp.where(source_of(flip, turn) < blk, 0.0, LOW_SCORE)
        return (number, base + 2 * HEAD_SIZE, lambda score: score + low)

    def block_tile(number, base):
        return (number, base + 2 * HEAD_SIZE, lambda score: score)

    def fold(groups, fresh_start):
        steps = []
        for tiles in groups:
            keys, values = [], []
            for number, base, _ in tiles:
                keys.append(chunks[number][base : base + HEAD_SIZE, :].T)
                value = chunks[number][base + HEAD_SIZE : base + 2 * HEAD_SIZE, :]
                values.append(jnp.concatenate([value, ones], axis=0))
            steps += [(head, keys, values, [close for _, _, close in tiles]) for head in range(HEADS)]

        def scores_of(head, keys, values, closes):
            return [
                close(dot(key, queries[head]) * LOG2_SCALE) for key, close in zip(keys, closes)
            ]

        tops, sums = [None] * HEADS, [None] * HEADS
        ahead = scores_of(*steps[0])
        for index, (head, keys, values, closes) in enumerate(steps):
            scores = ahead
            if index + 1 < len(steps):
                ahead = scores_of(*steps[index + 1])
            if index < HEADS and not fresh_start:
                source = (top_ref, sum_ref) if start is None else start
                tops[head], sums[head] = source[0][head, 0:1], source[1][head]
            top = jnp.max(functools.reduce(jnp.maximum, scores), axis=0, keepdims=True)
            before = tops[head]
            if before is not None:
                top = jnp.maximum(before, top)
            total = None
            for score, value in zip(scores, values):
                weight = jnp.exp2(score - top)
                high = weight.astype(BF16)
                low = (weight - high.astype(F32)).astype(BF16)
                part = dot(value, high) + dot(value, low)
                total = part if total is None else total + part
            if before is not None:
                total = sums[head] * jnp.exp2(before - top) + total
            tops[head], sums[head] = top, total
        for head in range(HEADS):
            sum_ref[head] = sums[head]
            top_ref[head] = jnp.broadcast_to(tops[head], (8, TOKENS))

    here, there, flipped = [], [], []
    for number, base, flip, turn in places:
        context = context_tile(number, base, flip, turn)
        if flip:
            there.append(context)
            flipped.append(block_tile(number, base))
        elif turn == 0:
            here.append([context, diagonal_tile(number, base)])
        else:
            here.append([context, masked_tile(number, base, flip, turn)])
    if len(there) == 1:
        here[-1] += there
    else:
        here.append(there)
    fold(here, first)
    start = None

    @pl.when(blk >= 4)
    def _():
        fold([flipped], False)

    if last:
        for head in range(HEADS):
            total = sum_ref[head]
            mixed = total[:HEAD_SIZE] / total[HEAD_SIZE : HEAD_SIZE + 1]
            out_ref[0, :, head * HEAD_SIZE : (head + 1) * HEAD_SIZE] = mixed.astype(BF16).T


def attend(block_offset, queries, chunks, places, state, last, token, early=()):
    first = state is None
    top, total = (HEADS, 8, TOKENS), (HEADS, HEAD_SIZE + TAIL, TOKENS)
    if last:
        outs = [shape((1, TOKENS, HEADS * HEAD_SIZE), BF16)]
        scratch = [pltpu.VMEM(top, F32), pltpu.VMEM(total, F32)]
    else:
        outs, scratch = [shape(top, F32), shape(total, F32)], []
    operands = [(block_offset, SMEM)]
    operands += [(a, VMEM) for a in (queries, *chunks, *(() if first else state), *early)]
    return run(
        functools.partial(attend_kernel, places, first, last, len(early)),
        "attend",
        24,
        token,
        outs,
        operands,
        scratch,
        cost=3,
    )


def pages_kernel(places, *refs):
    chunks, (mine_ref, other_ref) = refs[:-2], refs[-2:]
    instance = lax.axis_index("blk") * 2 + lax.axis_index("group")
    other = lax.axis_index("blk") * 2 + 1 - lax.axis_index("group")
    slots = 4 * PAGE_TOKENS
    row = lax.broadcasted_iota(jnp.int32, (slots, TOKENS), 0)
    lane = lax.broadcasted_iota(jnp.int32, (slots, TOKENS), 1)
    wanted = jnp.where(row < 2 * PAGE_TOKENS, instance * 2, other * 2) + row // PAGE_TOKENS % 2
    wanted = jnp.where(row % PAGE_TOKENS == lane % PAGE_TOKENS, wanted, -2).astype(F32)
    for number, base, flip, turn in places:
        source = source_of(flip, turn)
        chunk = chunks[number]
        codes = chunk[base + CHUNK : base + PIECE, :].astype(F32)[0:1]
        chooser = jnp.where(wanted == codes, 1.0, 0.0).astype(BF16)
        for part in range(2):
            start = base + (2 + part) * HEAD_SIZE
            found = dot_t(chooser, chunk[start : start + HEAD_SIZE, :]).astype(BF16)
            for rank in range(2):
                mine_ref[source, rank, part] = found[rank * PAGE_TOKENS : (rank + 1) * PAGE_TOKENS]
                other_ref[source, rank, part] = found[
                    (2 + rank) * PAGE_TOKENS : (3 + rank) * PAGE_TOKENS
                ]


def select_pages(chunks, places, token):
    out = shape((8, 2, 2, PAGE_TOKENS, HEAD_SIZE), BF16)
    return run(
        functools.partial(pages_kernel, places),
        "pages",
        8,
        token,
        [out, out],
        [(a, VMEM) for a in chunks],
    )


def pool_kernel(mine_ref, came_ref, out_ref):
    group = lax.axis_index("group")
    out_ref[:, group] = mine_ref[...]
    out_ref[:, 1 - group] = came_ref[...]


def pool(mine, came, token):
    out = shape((8, 2, 2, 2, PAGE_TOKENS, HEAD_SIZE), BF16)
    return run(pool_kernel, "pool", 4, token, [out], [(mine, VMEM), (came, VMEM)])


def attend_rows(
    length_ref, query_ref, step_ref, cache_ref, attended_ref, score_ref, mixed_ref, waits
):
    count = HEADS * STEPS * ROWS
    query = jnp.concatenate(
        [
            query_ref[0, :, :, h * HEAD_SIZE : (h + 1) * HEAD_SIZE].reshape(STEPS * ROWS, HEAD_SIZE)
            for h in range(HEADS)
        ],
        axis=0,
    )
    scaling = HEAD_SIZE**-0.5

    def row_of(width):
        return lax.broadcasted_iota(jnp.int32, (count, width), 0) % ROWS

    row_wide, row_head = row_of(LEN), row_of(HEAD_SIZE)
    lengths = jnp.zeros((count, LEN), jnp.int32)
    for r in range(ROWS):
        if r % (ROWS // 2) == 0:
            waits[r // (ROWS // 2)].wait()
        score = dot_t(query, cache_ref[0, 0, r])
        if r == 0:
            score_ref[...] = score
        else:
            score_ref[...] = jnp.where(row_wide == r, score, score_ref[...])
        lengths = jnp.where(row_wide == r, length_ref[0, r], lengths)
    live = lax.broadcasted_iota(jnp.int32, (count, LEN), 1) < lengths
    score_old = jnp.where(live, score_ref[...] * scaling, LOW_SCORE)
    new_keys = step_ref[0, :, 0].reshape(STEPS * ROWS, HEAD_SIZE)
    new_values = step_ref[0, :, 1].reshape(STEPS * ROWS, HEAD_SIZE)
    lane = lax.broadcasted_iota(jnp.int32, (count, STEPS * ROWS), 1)
    place = lax.broadcasted_iota(jnp.int32, (count, STEPS * ROWS), 0)
    open_new = (lane % ROWS == place % ROWS) & (lane // ROWS <= place // ROWS % STEPS)
    score_new = jnp.where(open_new, dot_t(query, new_keys) * scaling, LOW_SCORE)
    top = jnp.maximum(
        jnp.max(score_old, axis=1, keepdims=True), jnp.max(score_new, axis=1, keepdims=True)
    )
    weight_old = jnp.where(live, jnp.exp(score_old - top), 0.0)
    weight_new = jnp.where(open_new, jnp.exp(score_new - top), 0.0)
    totals = jnp.sum(weight_old, axis=1, keepdims=True) + jnp.sum(weight_new, axis=1, keepdims=True)
    rounded = weight_old.astype(BF16)
    for r in range(ROWS):
        if r % (ROWS // 2) == 0:
            waits[2 + r // (ROWS // 2)].wait()
        mixed = dot(rounded, cache_ref[0, 1, r])
        if r == 0:
            mixed_ref[...] = mixed
        else:
            mixed_ref[...] = jnp.where(row_head == r, mixed, mixed_ref[...])
    mixed = mixed_ref[...] + dot(weight_new.astype(BF16), new_values)
    attended = (mixed / totals).astype(BF16)
    for h in range(HEADS):
        attended_ref[:, h * HEAD_SIZE : (h + 1) * HEAD_SIZE] = attended[
            h * STEPS * ROWS : (h + 1) * STEPS * ROWS
        ]


TURNS = (2, 1, 3, 0)
SPLIT = 2
WIDTH = QUARTER // SPLIT


def decode_kernel(length_hbm, query_hbm, step_hbm, cache_hbm, weight_hbm, *refs):
    outs = refs[:4]
    length_ref, query_ref, step_ref, cache_ref, weight_ref = refs[4:9]
    attended_ref, score_ref, mixed_ref, row_sems, cache_sems, weight_sems = refs[9:]
    firsts = [
        pltpu.make_async_copy(query_hbm, query_ref, row_sems.at[0]),
        pltpu.make_async_copy(step_hbm, step_ref, row_sems.at[1]),
        pltpu.make_async_copy(length_hbm, length_ref, row_sems.at[2]),
    ]
    waits = []
    for number in range(4):
        rows = pl.ds(number % 2 * (ROWS // 2), ROWS // 2)
        waits.append(
            pltpu.make_async_copy(
                cache_hbm.at[0, number // 2, rows],
                cache_ref.at[0, number // 2, rows],
                cache_sems.at[number],
            )
        )
    y = lax.axis_index("tp") // 4
    copies = []
    for number in range(4 * SPLIT):
        column = (y + TURNS[number // SPLIT]) % 4 * QUARTER + number % SPLIT * WIDTH
        copies.append(
            pltpu.make_async_copy(
                weight_hbm.at[:, pl.ds(pl.multiple_of(column, WIDTH), WIDTH)],
                weight_ref.at[number],
                weight_sems.at[number],
            )
        )
    for copy in firsts + waits + copies:
        copy.start()
    for copy in firsts:
        copy.wait()
    attend_rows(
        length_ref, query_ref, step_ref, cache_ref, attended_ref, score_ref, mixed_ref, waits
    )
    attended = attended_ref[...]
    for number, copy in enumerate(copies):
        copy.wait()
        part = dot(attended, weight_ref[number])
        out = outs[number // SPLIT]
        columns = slice(number % SPLIT * WIDTH, (number % SPLIT + 1) * WIDTH)
        out[:, columns] = part.astype(out.dtype)


def decode(row_lengths, step_query, step_cache, row_cache, out_weight):
    rows = STEPS * ROWS
    operands = (row_lengths, step_query, step_cache, row_cache, out_weight)
    return run(
        decode_kernel,
        "decode",
        58,
        None,
        [shape((rows, QUARTER), BF16 if turn else F32) for turn in TURNS],
        [(a, pl.ANY) for a in operands],
        [
            pltpu.SMEM((1, ROWS), jnp.int32),
            pltpu.VMEM(step_query.shape, BF16),
            pltpu.VMEM(step_cache.shape, BF16),
            pltpu.VMEM(row_cache.shape, BF16),
            pltpu.VMEM((4 * SPLIT, out_weight.shape[0], WIDTH), BF16),
            pltpu.VMEM((rows, HEADS * HEAD_SIZE), BF16),
            pltpu.VMEM((HEADS * rows, LEN), F32),
            pltpu.VMEM((HEADS * rows, HEAD_SIZE), F32),
            pltpu.SemaphoreType.DMA((3,)),
            pltpu.SemaphoreType.DMA((4,)),
            pltpu.SemaphoreType.DMA((4 * SPLIT,)),
        ],
        cost=9,
    )


def quarter_kernel(own_ref, a_ref, b_ref, c_ref, *outs):
    z = lax.axis_index("tp") % 4
    for out, turn in zip(outs, TURNS):
        columns = pl.ds(pl.multiple_of((z + turn) % 4 * SHARE, SHARE), SHARE)
        out[...] = (
            own_ref[:, columns]
            + a_ref[:, columns].astype(F32)
            + b_ref[:, columns].astype(F32)
            + c_ref[:, columns].astype(F32)
        )


def sum_quarters(own, came, token):
    outs = [shape((STEPS * ROWS, SHARE), F32) for _ in TURNS]
    operands = [(a, VMEM) for a in (own, *came)]
    return run(quarter_kernel, "quarters", 4, token, outs, operands, cost=4)


def diagonal():
    rows = lax.broadcasted_iota(jnp.int32, (STEPS * ROWS, HEAD_SIZE), 0)
    return rows == lax.broadcasted_iota(jnp.int32, (STEPS * ROWS, HEAD_SIZE), 1)


def hidden_kernel(residual_ref, own_ref, a_ref, b_ref, c_ref, hidden_ref, square_ref):
    residual = residual_ref[0].reshape(STEPS * ROWS, SHARE).astype(F32)
    hidden = residual + (own_ref[...] + a_ref[...] + b_ref[...] + c_ref[...])
    hidden_ref[...] = hidden
    square = jnp.sum(hidden * hidden, axis=1, keepdims=True)
    square = jnp.sum(jnp.where(diagonal(), square, 0.0), axis=0, keepdims=True)
    square_ref[...] = jnp.broadcast_to(square[None], square_ref.shape)


def sum_shares(residual, own, came, token):
    outs = [shape((STEPS * ROWS, SHARE), F32), shape((16, 8, HEAD_SIZE), F32)]
    operands = [(a, VMEM) for a in (residual, own, *came)]
    return run(hidden_kernel, "hidden", 4, token, outs, operands)


def finish_kernel(hidden_ref, gain_ref, square_ref, out_ref):
    square = jnp.sum(square_ref[...], axis=0)[0:1]
    square = jnp.sum(jnp.where(diagonal(), square, 0.0), axis=1, keepdims=True)
    scale = lax.rsqrt(square * (1.0 / COLUMNS) + EPSILON)
    out = hidden_ref[...] * scale * gain_ref[...].reshape(1, SHARE).astype(F32)
    out_ref[0] = out.astype(BF16).reshape(STEPS, ROWS, SHARE)


def finish(hidden, gain, squares, token):
    outs = [shape((1, STEPS, ROWS, SHARE), BF16)]
    operands = [(a, VMEM) for a in (hidden, gain, squares)]
    return run(finish_kernel, "finish", 4, token, outs, operands)


def move_x(a, turn):
    return lax.ppermute(a, "blk", [(i, i // 4 * 4 + (i + turn) % 4) for i in range(8)])


def move_y(a, turn):
    return lax.ppermute(a, "tp", [(i, (i + 4 * turn) % 16) for i in range(16)])


def move_z(a, turn):
    return lax.ppermute(a, "tp", [(i, i // 4 * 4 + (i + turn) % 4) for i in range(16)])


def body(
    prompt_query,
    context_cache,
    new_block_cache,
    block_offset,
    page_owner,
    step_query,
    step_cache,
    row_cache,
    row_lengths,
    out_weight,
    residual,
    norm_gain,
):
    packed = pack(
        page_owner.reshape(1, PAGES),
        jnp.swapaxes(context_cache, 2, 3),
        jnp.swapaxes(new_block_cache, 2, 3),
    )
    near = lax.ppermute(packed, "tp", [(i, i ^ 1) for i in range(16)])
    far = lax.ppermute(packed, "blk", [(i, i ^ 4) for i in range(8)])
    *parts, own, token = decode(row_lengths, step_query, step_cache, row_cache, out_weight)
    far, parts[0] = lax.optimization_barrier((far, parts[0]))
    far_near = lax.ppermute(far, "tp", [(i, i ^ 1) for i in range(16)])
    came = [move_y(a, turn) for a, turn in zip(parts, TURNS)]
    here, token = join(packed, near, far, far_near, token)
    up = move_x(here, 1)
    down = move_x(here, 3)
    *state, token = attend(
        block_offset,
        prompt_query,
        [here],
        [(0, 0, 0, 0), (0, PIECE, 1, 0)],
        None,
        False,
        token,
        [own],
    )
    *shares, own, token = sum_quarters(own, came, token)
    came = [move_z(a, turn) for a, turn in zip(shares, TURNS)]
    up_two, down_two, token = relay(up, down, token)
    up_two = move_x(up_two, 1)
    down_two = move_x(down_two, 3)
    places = [(0, 0, 0, -1), (0, PIECE, 1, -1), (1, 0, 0, 1), (1, PIECE, 1, 1)]
    *state, token = attend(block_offset, prompt_query, [up, down], places, state, False, token)
    hidden, square, token = sum_shares(residual, own, came, token)
    squares = lax.all_to_all(square, "tp", split_axis=0, concat_axis=0, tiled=True)
    places = [(0, 0, 0, 0), (0, PIECE, 1, 0), (1, 0, 0, -1), (1, PIECE, 1, -1)]
    places += [(2, 0, 0, 1), (2, PIECE, 1, 1), (3, 0, 0, 2), (4, 0, 1, 2)]
    mine, other, token = select_pages([here, up, down, up_two, down_two], places, token)
    other = lax.ppermute(other, "group", [(0, 1), (1, 0)])
    prefill_out, token = attend(
        block_offset,
        prompt_query,
        [up_two, down_two],
        [(0, 0, 0, 2), (1, 0, 1, 2)],
        state,
        True,
        token,
    )
    page_pool, token = pool(mine, other, token)
    decode_out, token = finish(hidden, norm_gain, squares, token)
    return (prefill_out, page_pool.reshape(1, 32, 2, PAGE_TOKENS, HEAD_SIZE), decode_out)


def solution(mesh):
    placed = (
        P("group", "blk", "tp"),
        P("group", None, "blk", "tp"),
        P("group", None, "blk", "tp"),
        P(),
        P("group", "blk", None),
        P(("blk", "group"), None, None, "tp"),
        P(("blk", "group"), None, None, None, "tp"),
        P(("blk", "group"), None, None, None, "tp"),
        P(("blk", "group"), None),
        P("tp", None),
        P(("blk", "group"), None, None, "tp"),
        P("tp"),
    )
    return jax.shard_map(
        body,
        mesh=mesh,
        in_specs=placed,
        out_specs=(
            P("group", "blk", "tp"),
            P(("blk", "group"), None, None, None, "tp"),
            P(("blk", "group"), None, None, "tp"),
        ),
        check_vma=False,
    )
```

```python
import functools
import math

import jax
import jax.numpy as jnp
from jax import lax
from jax.experimental import pallas as pl
from jax.experimental.pallas import tpu as pltpu
from jax.sharding import PartitionSpec as P

HEAD_SIZE = 128
PAGE_TOKENS = 16
STEPS = 4
ROWS = 16
LEN = 256
HEADS = 4
TOKENS = 256
PAGES = TOKENS // PAGE_TOKENS
HALF = HEAD_SIZE // 2
PACKED = 4 * HALF
CHUNK = 4 * HEAD_SIZE
TAIL = 16
PIECE = CHUNK + TAIL
COLUMNS = 8192
QUARTER = COLUMNS // 4
SHARE = COLUMNS // 16
LOW_SCORE = -1e30
EPSILON = 1e-05
F32 = jnp.float32
BF16 = jnp.bfloat16
LOG2_SCALE = math.log2(math.e) * HEAD_SIZE**-0.5
VMEM = pltpu.VMEM
SMEM = pltpu.SMEM
MIB = 1024 * 1024
WHOLE = 60


def params(mebibytes):
    return pltpu.CompilerParams(vmem_limit_bytes=int(mebibytes * MIB))


def spec(space=VMEM):
    return pl.BlockSpec(memory_space=space)


def shape(dims, dtype):
    return jax.ShapeDtypeStruct(dims, dtype)


def dot_t(a, b):
    return lax.dot_general(a, b, (((1,), (1,)), ((), ())), preferred_element_type=F32)


def dot(a, b):
    return lax.dot_general(a, b, (((1,), (0,)), ((), ())), preferred_element_type=F32)


TOKEN = shape((8, HEAD_SIZE), F32)


def run(kernel, title, mebibytes, token, outs, operands, scratch=(), emit=True, cost=0, space=VMEM):
    tokens = [] if token is None else [token]
    count = len(operands) + len(tokens)

    def with_token(*refs):
        results, rest = refs[count : count + len(outs)], refs[count + len(outs) :]
        if emit:
            gone, *rest = rest
            gone[...] = refs[len(operands)][...] if tokens else jnp.zeros(gone.shape, gone.dtype)
        kernel(*refs[: len(operands)], *results, *rest)

    return pl.pallas_call(
        with_token,
        out_shape=(*outs, TOKEN) if emit else tuple(outs),
        in_specs=[spec(space) for _, space in operands] + [spec()] * len(tokens),
        out_specs=(spec(space),) * len(outs) + (spec(),) * emit,
        scratch_shapes=list(scratch),
        compiler_params=params(mebibytes),
        cost_estimate=pl.CostEstimate(
            flops=1024 + 1150000000 * cost, bytes_accessed=1024, transcendentals=0
        ),
        name=title,
    )(*[a for a, _ in operands], *tokens)


def pack_kernel(owner_hbm, context_hbm, block_hbm, out_ref, owner_ref, sems):
    copies = [pltpu.make_async_copy(owner_hbm, owner_ref, sems.at[4])]
    for number in range(4):
        source = context_hbm if number < 2 else block_hbm
        copies.append(
            pltpu.make_async_copy(
                source.at[0, number % 2],
                out_ref.at[pl.ds(number * HALF, HALF), :],
                sems.at[number],
            )
        )
    for copy in copies:
        copy.start()
    copies[0].wait()
    owners = [owner_ref[0, p] for p in range(PAGES)]
    page = lax.broadcasted_iota(jnp.int32, (TAIL, TOKENS), 1) // PAGE_TOKENS
    codes = jnp.full((TAIL, TOKENS), -1, jnp.int32)
    for p in range(PAGES):
        rank = jnp.int32(0)
        for q in range(p):
            rank = rank + (owners[q] == owners[p]).astype(jnp.int32)
        codes = jnp.where(page == p, owners[p] * 2 + rank, codes)
    out_ref[PACKED:, :] = codes.astype(F32).astype(BF16)
    for copy in copies[1:]:
        copy.wait()


def pack(page_owner, context_cache, new_block_cache):
    return run(
        pack_kernel,
        "pack",
        WHOLE,
        None,
        [shape((PACKED + TAIL, TOKENS), BF16)],
        [(a, pl.ANY) for a in (page_owner, context_cache, new_block_cache)],
        [pltpu.SMEM((1, PAGES), jnp.int32), pltpu.SemaphoreType.DMA((5,))],
        emit=False,
    )[0]


def join_kernel(mine_ref, near_ref, far_ref, far_near_ref, out_ref):
    odd = lax.axis_index("tp") % 2
    for base, first_ref, second_ref in ((0, mine_ref, near_ref), (PIECE, far_ref, far_near_ref)):
        for number in range(4):
            rows = slice(number * HALF, (number + 1) * HALF)
            here = pl.multiple_of(base + number * HEAD_SIZE + odd * HALF, 16)
            there = pl.multiple_of(base + number * HEAD_SIZE + (1 - odd) * HALF, 16)
            out_ref[pl.ds(here, HALF), :] = first_ref[rows, :]
            out_ref[pl.ds(there, HALF), :] = second_ref[rows, :]
        out_ref[base + CHUNK : base + PIECE, :] = first_ref[PACKED:, :]


def join(mine, near, far, far_near, token):
    outs = [shape((2 * PIECE, TOKENS), BF16)]
    operands = [(a, VMEM) for a in (mine, near, far, far_near)]
    return run(join_kernel, "join", 4, token, outs, operands)


def relay_kernel(up_ref, down_ref, up_out, down_out):
    up_out[...] = up_ref[:PIECE, :]
    down_out[...] = down_ref[PIECE:, :]


def relay(up, down, token):
    outs = [shape((PIECE, TOKENS), BF16)] * 2
    operands = [(up, VMEM), (down, VMEM)]
    return run(relay_kernel, "relay", 4, token, outs, operands, cost=2)


def source_of(flip, turn):
    blk = lax.axis_index("blk")
    return (blk // 4 + flip) % 2 * 4 + (blk % 4 + turn + 4) % 4


def attend_kernel(places, first, last, early, *refs):
    offset_ref, query_ref = refs[:2]
    arrays = 1 + max(place[0] for place in places)
    chunks = refs[2 : 2 + arrays]
    refs = refs[2 + arrays :]
    start = None
    if not first:
        start = refs[:2]
        refs = refs[2:]
    refs = refs[early:]
    if last:
        out_ref, *refs = refs
    top_ref, sum_ref = refs
    blk = lax.axis_index("blk")
    offset = offset_ref[lax.axis_index("group")]
    key_number = lax.broadcasted_iota(jnp.int32, (TOKENS, TOKENS), 0)
    query_number = lax.broadcasted_iota(jnp.int32, (TOKENS, TOKENS), 1)
    queries = [query_ref[0, :, h * HEAD_SIZE : (h + 1) * HEAD_SIZE].T for h in range(HEADS)]
    ones = jnp.ones((TAIL, TOKENS), BF16)

    def context_tile(number, base, flip, turn):
        start = source_of(flip, turn) * TOKENS
        bias = jnp.where(start + key_number < offset, 0.0, LOW_SCORE)
        return (number, base, lambda score: score + bias)

    def diagonal_tile(number, base):
        low = jnp.where(key_number <= query_number, 0.0, LOW_SCORE)
        return (number, base + 2 * HEAD_SIZE, lambda score: score + low)

    def masked_tile(number, base, flip, turn):
        low = jnp.where(source_of(flip, turn) < blk, 0.0, LOW_SCORE)
        return (number, base + 2 * HEAD_SIZE, lambda score: score + low)

    def block_tile(number, base):
        return (number, base + 2 * HEAD_SIZE, lambda score: score)

    def fold(groups, fresh_start):
        steps = []
        for tiles in groups:
            keys, values = [], []
            for number, base, _ in tiles:
                keys.append(chunks[number][base : base + HEAD_SIZE, :].T)
                value = chunks[number][base + HEAD_SIZE : base + 2 * HEAD_SIZE, :]
                values.append(jnp.concatenate([value, ones], axis=0))
            steps += [(head, keys, values, [close for _, _, close in tiles]) for head in range(HEADS)]

        def scores_of(head, keys, values, closes):
            return [
                close(dot(key, queries[head]) * LOG2_SCALE) for key, close in zip(keys, closes)
            ]

        tops, sums = [None] * HEADS, [None] * HEADS
        ahead = scores_of(*steps[0])
        for index, (head, keys, values, closes) in enumerate(steps):
            scores = ahead
            if index + 1 < len(steps):
                ahead = scores_of(*steps[index + 1])
            if index < HEADS and not fresh_start:
                source = (top_ref, sum_ref) if start is None else start
                tops[head], sums[head] = source[0][head, 0:1], source[1][head]
            top = jnp.max(functools.reduce(jnp.maximum, scores), axis=0, keepdims=True)
            before = tops[head]
            if before is not None:
                top = jnp.maximum(before, top)
            total = None
            for score, value in zip(scores, values):
                weight = jnp.exp2(score - top)
                high = weight.astype(BF16)
                low = (weight - high.astype(F32)).astype(BF16)
                part = dot(value, high) + dot(value, low)
                total = part if total is None else total + part
            if before is not None:
                total = sums[head] * jnp.exp2(before - top) + total
            tops[head], sums[head] = top, total
        for head in range(HEADS):
            sum_ref[head] = sums[head]
            top_ref[head] = jnp.broadcast_to(tops[head], (8, TOKENS))

    here, there, flipped = [], [], []
    for number, base, flip, turn in places:
        context = context_tile(number, base, flip, turn)
        if flip:
            there.append(context)
            flipped.append(block_tile(number, base))
        elif turn == 0:
            here.append([context, diagonal_tile(number, base)])
        else:
            here.append([context, masked_tile(number, base, flip, turn)])
    if len(there) == 1:
        here[-1] += there
    else:
        here.append(there)
    fold(here, first)
    start = None

    @pl.when(blk >= 4)
    def _():
        fold([flipped], False)

    if last:
        for head in range(HEADS):
            total = sum_ref[head]
            mixed = total[:HEAD_SIZE] / total[HEAD_SIZE : HEAD_SIZE + 1]
            out_ref[0, :, head * HEAD_SIZE : (head + 1) * HEAD_SIZE] = mixed.astype(BF16).T


def attend(block_offset, queries, chunks, places, state, last, token, early=()):
    first = state is None
    top, total = (HEADS, 8, TOKENS), (HEADS, HEAD_SIZE + TAIL, TOKENS)
    if last:
        outs = [shape((1, TOKENS, HEADS * HEAD_SIZE), BF16)]
        scratch = [pltpu.VMEM(top, F32), pltpu.VMEM(total, F32)]
    else:
        outs, scratch = [shape(top, F32), shape(total, F32)], []
    operands = [(block_offset, SMEM)]
    operands += [(a, VMEM) for a in (queries, *chunks, *(() if first else state), *early)]
    return run(
        functools.partial(attend_kernel, places, first, last, len(early)),
        "attend",
        24,
        token,
        outs,
        operands,
        scratch,
        cost=3,
    )


def pages_kernel(places, *refs):
    chunks, (mine_ref, other_ref) = refs[:-2], refs[-2:]
    instance = lax.axis_index("blk") * 2 + lax.axis_index("group")
    other = lax.axis_index("blk") * 2 + 1 - lax.axis_index("group")
    slots = 4 * PAGE_TOKENS
    row = lax.broadcasted_iota(jnp.int32, (slots, TOKENS), 0)
    lane = lax.broadcasted_iota(jnp.int32, (slots, TOKENS), 1)
    wanted = jnp.where(row < 2 * PAGE_TOKENS, instance * 2, other * 2) + row // PAGE_TOKENS % 2
    wanted = jnp.where(row % PAGE_TOKENS == lane % PAGE_TOKENS, wanted, -2).astype(F32)
    for number, base, flip, turn in places:
        source = source_of(flip, turn)
        chunk = chunks[number]
        codes = chunk[base + CHUNK : base + PIECE, :].astype(F32)[0:1]
        chooser = jnp.where(wanted == codes, 1.0, 0.0).astype(BF16)
        for part in range(2):
            start = base + (2 + part) * HEAD_SIZE
            found = dot_t(chooser, chunk[start : start + HEAD_SIZE, :]).astype(BF16)
            for rank in range(2):
                mine_ref[source, rank, part] = found[rank * PAGE_TOKENS : (rank + 1) * PAGE_TOKENS]
                other_ref[source, rank, part] = found[
                    (2 + rank) * PAGE_TOKENS : (3 + rank) * PAGE_TOKENS
                ]


def select_pages(chunks, places, token):
    out = shape((8, 2, 2, PAGE_TOKENS, HEAD_SIZE), BF16)
    return run(
        functools.partial(pages_kernel, places),
        "pages",
        8,
        token,
        [out, out],
        [(a, VMEM) for a in chunks],
    )


def pool_kernel(mine_ref, came_ref, out_ref):
    group = lax.axis_index("group")
    out_ref[:, group] = mine_ref[...]
    out_ref[:, 1 - group] = came_ref[...]


def pool(mine, came, token):
    out = shape((8, 2, 2, 2, PAGE_TOKENS, HEAD_SIZE), BF16)
    return run(pool_kernel, "pool", 4, token, [out], [(mine, VMEM), (came, VMEM)])


def attend_rows(
    length_ref, query_ref, step_ref, cache_ref, attended_ref, score_ref, mixed_ref, waits
):
    count = HEADS * STEPS * ROWS
    query = jnp.concatenate(
        [
            query_ref[0, :, :, h * HEAD_SIZE : (h + 1) * HEAD_SIZE].reshape(STEPS * ROWS, HEAD_SIZE)
            for h in range(HEADS)
        ],
        axis=0,
    )
    scaling = HEAD_SIZE**-0.5

    def row_of(width):
        return lax.broadcasted_iota(jnp.int32, (count, width), 0) % ROWS

    row_wide, row_head = row_of(LEN), row_of(HEAD_SIZE)
    lengths = jnp.zeros((count, LEN), jnp.int32)
    for r in range(ROWS):
        if r % (ROWS // 2) == 0:
            waits[r // (ROWS // 2)].wait()
        score = dot_t(query, cache_ref[0, 0, r])
        if r == 0:
            score_ref[...] = score
        else:
            score_ref[...] = jnp.where(row_wide == r, score, score_ref[...])
        lengths = jnp.where(row_wide == r, length_ref[0, r], lengths)
    live = lax.broadcasted_iota(jnp.int32, (count, LEN), 1) < lengths
    score_old = jnp.where(live, score_ref[...] * scaling, LOW_SCORE)
    new_keys = step_ref[0, :, 0].reshape(STEPS * ROWS, HEAD_SIZE)
    new_values = step_ref[0, :, 1].reshape(STEPS * ROWS, HEAD_SIZE)
    lane = lax.broadcasted_iota(jnp.int32, (count, STEPS * ROWS), 1)
    place = lax.broadcasted_iota(jnp.int32, (count, STEPS * ROWS), 0)
    open_new = (lane % ROWS == place % ROWS) & (lane // ROWS <= place // ROWS % STEPS)
    score_new = jnp.where(open_new, dot_t(query, new_keys) * scaling, LOW_SCORE)
    top = jnp.maximum(
        jnp.max(score_old, axis=1, keepdims=True), jnp.max(score_new, axis=1, keepdims=True)
    )
    weight_old = jnp.where(live, jnp.exp(score_old - top), 0.0)
    weight_new = jnp.where(open_new, jnp.exp(score_new - top), 0.0)
    totals = jnp.sum(weight_old, axis=1, keepdims=True) + jnp.sum(weight_new, axis=1, keepdims=True)
    rounded = weight_old.astype(BF16)
    for r in range(ROWS):
        if r % (ROWS // 2) == 0:
            waits[2 + r // (ROWS // 2)].wait()
        mixed = dot(rounded, cache_ref[0, 1, r])
        if r == 0:
            mixed_ref[...] = mixed
        else:
            mixed_ref[...] = jnp.where(row_head == r, mixed, mixed_ref[...])
    mixed = mixed_ref[...] + dot(weight_new.astype(BF16), new_values)
    attended = (mixed / totals).astype(BF16)
    for h in range(HEADS):
        attended_ref[:, h * HEAD_SIZE : (h + 1) * HEAD_SIZE] = attended[
            h * STEPS * ROWS : (h + 1) * STEPS * ROWS
        ]


TURNS = (2, 1, 3, 0)
ORDER = (0, 2, 1, 3)
SPLIT = 2
WIDTH = QUARTER // SPLIT


def decode_kernel(length_hbm, query_hbm, step_hbm, cache_hbm, weight_hbm, *refs):
    outs = refs[:4]
    length_ref, query_ref, step_ref, cache_ref, weight_ref, own_ref, part_ref = refs[4:11]
    attended_ref, score_ref, mixed_ref, row_sems, cache_sems, weight_sems, out_sems = refs[11:]
    firsts = [
        pltpu.make_async_copy(query_hbm, query_ref, row_sems.at[0]),
        pltpu.make_async_copy(step_hbm, step_ref, row_sems.at[1]),
        pltpu.make_async_copy(length_hbm, length_ref, row_sems.at[2]),
    ]
    waits = []
    for number in range(4):
        rows = pl.ds(number % 2 * (ROWS // 2), ROWS // 2)
        waits.append(
            pltpu.make_async_copy(
                cache_hbm.at[0, number // 2, rows],
                cache_ref.at[0, number // 2, rows],
                cache_sems.at[number],
            )
        )
    y = lax.axis_index("tp") // 4
    copies = []
    for number in range(4 * SPLIT):
        column = (y + ORDER[number // SPLIT]) % 4 * QUARTER + number % SPLIT * WIDTH
        copies.append(
            pltpu.make_async_copy(
                weight_hbm.at[:, pl.ds(pl.multiple_of(column, WIDTH), WIDTH)],
                weight_ref.at[number],
                weight_sems.at[number],
            )
        )
    for copy in firsts + waits + copies:
        copy.start()
    for copy in firsts:
        copy.wait()
    attend_rows(
        length_ref, query_ref, step_ref, cache_ref, attended_ref, score_ref, mixed_ref, waits
    )
    attended = attended_ref[...]
    leaving = []
    for number, copy in enumerate(copies):
        copy.wait()
        part = dot(attended, weight_ref[number])
        quarter = number // SPLIT
        columns = slice(number % SPLIT * WIDTH, (number % SPLIT + 1) * WIDTH)
        if quarter == 0:
            own_ref[:, columns] = part
        else:
            part_ref[quarter - 1, :, columns] = part.astype(BF16)
        if number % SPLIT == SPLIT - 1:
            source = own_ref if quarter == 0 else part_ref.at[quarter - 1]
            leaving.append(pltpu.make_async_copy(source, outs[quarter], out_sems.at[quarter]))
            leaving[-1].start()
    for copy in leaving:
        copy.wait()


def decode(row_lengths, step_query, step_cache, row_cache, out_weight):
    rows = STEPS * ROWS
    operands = (row_lengths, step_query, step_cache, row_cache, out_weight)
    return run(
        decode_kernel,
        "decode",
        58,
        None,
        [shape((rows, QUARTER), BF16 if turn else F32) for turn in ORDER],
        [(a, pl.ANY) for a in operands],
        [
            pltpu.SMEM((1, ROWS), jnp.int32),
            pltpu.VMEM(step_query.shape, BF16),
            pltpu.VMEM(step_cache.shape, BF16),
            pltpu.VMEM(row_cache.shape, BF16),
            pltpu.VMEM((4 * SPLIT, out_weight.shape[0], WIDTH), BF16),
            pltpu.VMEM((rows, QUARTER), F32),
            pltpu.VMEM((3, rows, QUARTER), BF16),
            pltpu.VMEM((rows, HEADS * HEAD_SIZE), BF16),
            pltpu.VMEM((HEADS * rows, LEN), F32),
            pltpu.VMEM((HEADS * rows, HEAD_SIZE), F32),
            pltpu.SemaphoreType.DMA((3,)),
            pltpu.SemaphoreType.DMA((4,)),
            pltpu.SemaphoreType.DMA((4 * SPLIT,)),
            pltpu.SemaphoreType.DMA((4,)),
        ],
        cost=9,
        emit=False,
        space=pl.ANY,
    )


def quarter_kernel(own_ref, a_ref, b_ref, c_ref, *outs):
    z = lax.axis_index("tp") % 4
    for out, turn in zip(outs, TURNS):
        columns = pl.ds(pl.multiple_of((z + turn) % 4 * SHARE, SHARE), SHARE)
        total = (
            own_ref[:, columns]
            + a_ref[:, columns].astype(F32)
            + b_ref[:, columns].astype(F32)
            + c_ref[:, columns].astype(F32)
        )
        out[...] = total.astype(out.dtype)


def sum_quarters(own, came, token):
    outs = [shape((STEPS * ROWS, SHARE), BF16 if turn == 2 else F32) for turn in TURNS]
    operands = [(a, VMEM) for a in (own, *came)]
    return run(quarter_kernel, "quarters", 4, token, outs, operands, cost=4)


def diagonal():
    rows = lax.broadcasted_iota(jnp.int32, (STEPS * ROWS, HEAD_SIZE), 0)
    return rows == lax.broadcasted_iota(jnp.int32, (STEPS * ROWS, HEAD_SIZE), 1)


def hidden_kernel(residual_ref, own_ref, a_ref, b_ref, c_ref, hidden_ref, square_ref):
    residual = residual_ref[0].reshape(STEPS * ROWS, SHARE).astype(F32)
    hidden = residual + (
        own_ref[...] + a_ref[...].astype(F32) + b_ref[...] + c_ref[...]
    )
    hidden_ref[...] = hidden
    square = jnp.sum(hidden * hidden, axis=1, keepdims=True)
    square = jnp.sum(jnp.where(diagonal(), square, 0.0), axis=0, keepdims=True)
    square_ref[...] = jnp.broadcast_to(square[None], square_ref.shape)


def sum_shares(residual, own, came, token):
    outs = [shape((STEPS * ROWS, SHARE), F32), shape((16, 8, HEAD_SIZE), F32)]
    operands = [(a, VMEM) for a in (residual, own, *came)]
    return run(hidden_kernel, "hidden", 4, token, outs, operands, cost=4)


def finish_kernel(hidden_ref, gain_ref, square_ref, out_ref):
    square = jnp.sum(square_ref[...], axis=0)[0:1]
    square = jnp.sum(jnp.where(diagonal(), square, 0.0), axis=1, keepdims=True)
    scale = lax.rsqrt(square * (1.0 / COLUMNS) + EPSILON)
    out = hidden_ref[...] * scale * gain_ref[...].reshape(1, SHARE).astype(F32)
    out_ref[0] = out.astype(BF16).reshape(STEPS, ROWS, SHARE)


def finish(hidden, gain, squares, token):
    outs = [shape((1, STEPS, ROWS, SHARE), BF16)]
    operands = [(a, VMEM) for a in (hidden, gain, squares)]
    return run(finish_kernel, "finish", 4, token, outs, operands)


def move_x(a, turn):
    return lax.ppermute(a, "blk", [(i, i // 4 * 4 + (i + turn) % 4) for i in range(8)])


def move_y(a, turn):
    return lax.ppermute(a, "tp", [(i, (i + 4 * turn) % 16) for i in range(16)])


def move_z(a, turn):
    return lax.ppermute(a, "tp", [(i, i // 4 * 4 + (i + turn) % 4) for i in range(16)])


def body(
    prompt_query,
    context_cache,
    new_block_cache,
    block_offset,
    page_owner,
    step_query,
    step_cache,
    row_cache,
    row_lengths,
    out_weight,
    residual,
    norm_gain,
):
    packed = pack(
        page_owner.reshape(1, PAGES),
        jnp.swapaxes(context_cache, 2, 3),
        jnp.swapaxes(new_block_cache, 2, 3),
    )
    near = lax.ppermute(packed, "tp", [(i, i ^ 1) for i in range(16)])
    far = lax.ppermute(packed, "blk", [(i, i ^ 4) for i in range(8)])
    own, *parts = decode(row_lengths, step_query, step_cache, row_cache, out_weight)
    far, parts[0] = lax.optimization_barrier((far, parts[0]))
    far_near = lax.ppermute(far, "tp", [(i, i ^ 1) for i in range(16)])
    came = [move_y(a, turn) for a, turn in zip(parts, TURNS)]
    here, token = join(packed, near, far, far_near, None)
    up = move_x(here, 1)
    down = move_x(here, 3)
    *state, token = attend(
        block_offset,
        prompt_query,
        [here],
        [(0, 0, 0, 0), (0, PIECE, 1, 0)],
        None,
        False,
        token,
        [own],
    )
    *shares, own, token = sum_quarters(own, came, token)
    came = [move_z(a, turn) for a, turn in zip(shares, TURNS)]
    places = [(0, 0, 0, -1), (0, PIECE, 1, -1)]
    *state, token = attend(block_offset, prompt_query, [up], places, state, False, token)
    up_two, down_two, token = relay(up, down, token)
    up_two = move_x(up_two, 1)
    down_two = move_x(down_two, 3)
    hidden, square, token = sum_shares(residual, own, came, token)
    squares = lax.all_to_all(square, "tp", split_axis=0, concat_axis=0, tiled=True)
    places = [(0, 0, 0, 0), (0, PIECE, 1, 0), (1, 0, 0, -1), (1, PIECE, 1, -1)]
    places += [(2, 0, 0, 1), (2, PIECE, 1, 1), (3, 0, 0, 2), (4, 0, 1, 2)]
    mine, other, token = select_pages([here, up, down, up_two, down_two], places, token)
    other = lax.ppermute(other, "group", [(0, 1), (1, 0)])
    prefill_out, token = attend(
        block_offset,
        prompt_query,
        [down, up_two, down_two],
        [(0, 0, 0, 1), (0, PIECE, 1, 1), (1, 0, 0, 2), (2, 0, 1, 2)],
        state,
        True,
        token,
    )
    page_pool, token = pool(mine, other, token)
    decode_out, token = finish(hidden, norm_gain, squares, token)
    return (prefill_out, page_pool.reshape(1, 32, 2, PAGE_TOKENS, HEAD_SIZE), decode_out)


def solution(mesh):
    placed = (
        P("group", "blk", "tp"),
        P("group", None, "blk", "tp"),
        P("group", None, "blk", "tp"),
        P(),
        P("group", "blk", None),
        P(("blk", "group"), None, None, "tp"),
        P(("blk", "group"), None, None, None, "tp"),
        P(("blk", "group"), None, None, None, "tp"),
        P(("blk", "group"), None),
        P("tp", None),
        P(("blk", "group"), None, None, "tp"),
        P("tp"),
    )
    return jax.shard_map(
        body,
        mesh=mesh,
        in_specs=placed,
        out_specs=(
            P("group", "blk", "tp"),
            P(("blk", "group"), None, None, None, "tp"),
            P(("blk", "group"), None, None, "tp"),
        ),
        check_vma=False,
    )
```

```python
import functools
import math

import jax
import jax.numpy as jnp
from jax import lax
from jax.experimental import pallas as pl
from jax.experimental.pallas import tpu as pltpu
from jax.sharding import PartitionSpec as P

HEAD_SIZE = 128
PAGE_TOKENS = 16
STEPS = 4
ROWS = 16
LEN = 256
HEADS = 4
TOKENS = 256
PAGES = TOKENS // PAGE_TOKENS
HALF = HEAD_SIZE // 2
PACKED = 4 * HALF
CHUNK = 4 * HEAD_SIZE
TAIL = 16
PIECE = CHUNK + TAIL
COLUMNS = 8192
QUARTER = COLUMNS // 4
SHARE = COLUMNS // 16
LOW_SCORE = -1e30
EPSILON = 1e-05
F32 = jnp.float32
BF16 = jnp.bfloat16
LOG2_SCALE = math.log2(math.e) * HEAD_SIZE**-0.5
VMEM = pltpu.VMEM
SMEM = pltpu.SMEM
MIB = 1024 * 1024
WHOLE = 60


def params(mebibytes):
    return pltpu.CompilerParams(vmem_limit_bytes=int(mebibytes * MIB))


def spec(space=VMEM):
    return pl.BlockSpec(memory_space=space)


def shape(dims, dtype):
    return jax.ShapeDtypeStruct(dims, dtype)


def dot_t(a, b):
    return lax.dot_general(a, b, (((1,), (1,)), ((), ())), preferred_element_type=F32)


def dot(a, b):
    return lax.dot_general(a, b, (((1,), (0,)), ((), ())), preferred_element_type=F32)


TOKEN = shape((8, HEAD_SIZE), F32)


def run(kernel, title, mebibytes, token, outs, operands, scratch=(), emit=True, cost=0, space=VMEM):
    tokens = [] if token is None else [token]
    count = len(operands) + len(tokens)

    def with_token(*refs):
        results, rest = refs[count : count + len(outs)], refs[count + len(outs) :]
        if emit:
            gone, *rest = rest
            gone[...] = refs[len(operands)][...] if tokens else jnp.zeros(gone.shape, gone.dtype)
        kernel(*refs[: len(operands)], *results, *rest)

    return pl.pallas_call(
        with_token,
        out_shape=(*outs, TOKEN) if emit else tuple(outs),
        in_specs=[spec(space) for _, space in operands] + [spec()] * len(tokens),
        out_specs=(spec(space),) * len(outs) + (spec(),) * emit,
        scratch_shapes=list(scratch),
        compiler_params=params(mebibytes),
        cost_estimate=pl.CostEstimate(
            flops=1024 + 1150000000 * cost, bytes_accessed=1024, transcendentals=0
        ),
        name=title,
    )(*[a for a, _ in operands], *tokens)


def pack_kernel(owner_hbm, context_hbm, block_hbm, out_ref, owner_ref, sems):
    copies = [pltpu.make_async_copy(owner_hbm, owner_ref, sems.at[4])]
    for number in range(4):
        source = context_hbm if number < 2 else block_hbm
        copies.append(
            pltpu.make_async_copy(
                source.at[0, number % 2],
                out_ref.at[pl.ds(number * HALF, HALF), :],
                sems.at[number],
            )
        )
    for copy in copies:
        copy.start()
    copies[0].wait()
    owners = [owner_ref[0, p] for p in range(PAGES)]
    page = lax.broadcasted_iota(jnp.int32, (TAIL, TOKENS), 1) // PAGE_TOKENS
    codes = jnp.full((TAIL, TOKENS), -1, jnp.int32)
    for p in range(PAGES):
        rank = jnp.int32(0)
        for q in range(p):
            rank = rank + (owners[q] == owners[p]).astype(jnp.int32)
        codes = jnp.where(page == p, owners[p] * 2 + rank, codes)
    out_ref[PACKED:, :] = codes.astype(F32).astype(BF16)
    for copy in copies[1:]:
        copy.wait()


def pack(page_owner, context_cache, new_block_cache):
    return run(
        pack_kernel,
        "pack",
        WHOLE,
        None,
        [shape((PACKED + TAIL, TOKENS), BF16)],
        [(a, pl.ANY) for a in (page_owner, context_cache, new_block_cache)],
        [pltpu.SMEM((1, PAGES), jnp.int32), pltpu.SemaphoreType.DMA((5,))],
        emit=False,
    )[0]


def join_kernel(mine_ref, near_ref, far_ref, far_near_ref, out_ref):
    odd = lax.axis_index("tp") % 2
    for base, first_ref, second_ref in ((0, mine_ref, near_ref), (PIECE, far_ref, far_near_ref)):
        for number in range(4):
            rows = slice(number * HALF, (number + 1) * HALF)
            here = pl.multiple_of(base + number * HEAD_SIZE + odd * HALF, 16)
            there = pl.multiple_of(base + number * HEAD_SIZE + (1 - odd) * HALF, 16)
            out_ref[pl.ds(here, HALF), :] = first_ref[rows, :]
            out_ref[pl.ds(there, HALF), :] = second_ref[rows, :]
        out_ref[base + CHUNK : base + PIECE, :] = first_ref[PACKED:, :]


def join(mine, near, far, far_near, token):
    outs = [shape((2 * PIECE, TOKENS), BF16)]
    operands = [(a, VMEM) for a in (mine, near, far, far_near)]
    return run(join_kernel, "join", 4, token, outs, operands)


def relay_kernel(up_ref, down_ref, up_out, down_out):
    up_out[...] = up_ref[:PIECE, :]
    down_out[...] = down_ref[PIECE:, :]


def relay(up, down, token):
    outs = [shape((PIECE, TOKENS), BF16)] * 2
    operands = [(up, VMEM), (down, VMEM)]
    return run(relay_kernel, "relay", 4, token, outs, operands, cost=2)


def source_of(flip, turn):
    blk = lax.axis_index("blk")
    return (blk // 4 + flip) % 2 * 4 + (blk % 4 + turn + 4) % 4


def attend_kernel(places, first, last, early, *refs):
    offset_ref, query_ref = refs[:2]
    arrays = 1 + max(place[0] for place in places)
    chunks = refs[2 : 2 + arrays]
    refs = refs[2 + arrays :]
    start = None
    if not first:
        start = refs[:2]
        refs = refs[2:]
    refs = refs[early:]
    if last:
        out_ref, *refs = refs
    top_ref, sum_ref = refs
    blk = lax.axis_index("blk")
    offset = offset_ref[lax.axis_index("group")]
    key_number = lax.broadcasted_iota(jnp.int32, (TOKENS, TOKENS), 0)
    query_number = lax.broadcasted_iota(jnp.int32, (TOKENS, TOKENS), 1)
    queries = [query_ref[0, :, h * HEAD_SIZE : (h + 1) * HEAD_SIZE].T for h in range(HEADS)]
    ones = jnp.ones((TAIL, TOKENS), BF16)

    def context_tile(number, base, flip, turn):
        start = source_of(flip, turn) * TOKENS
        bias = jnp.where(start + key_number < offset, 0.0, LOW_SCORE)
        return (number, base, lambda score: score + bias)

    def diagonal_tile(number, base):
        low = jnp.where(key_number <= query_number, 0.0, LOW_SCORE)
        return (number, base + 2 * HEAD_SIZE, lambda score: score + low)

    def masked_tile(number, base, flip, turn):
        low = jnp.where(source_of(flip, turn) < blk, 0.0, LOW_SCORE)
        return (number, base + 2 * HEAD_SIZE, lambda score: score + low)

    def block_tile(number, base):
        return (number, base + 2 * HEAD_SIZE, lambda score: score)

    def fold(groups, fresh_start):
        steps = []
        for tiles in groups:
            keys, values = [], []
            for number, base, _ in tiles:
                keys.append(chunks[number][base : base + HEAD_SIZE, :].T)
                value = chunks[number][base + HEAD_SIZE : base + 2 * HEAD_SIZE, :]
                values.append(jnp.concatenate([value, ones], axis=0))
            steps += [(head, keys, values, [close for _, _, close in tiles]) for head in range(HEADS)]

        def scores_of(head, keys, values, closes):
            return [
                close(dot(key, queries[head]) * LOG2_SCALE) for key, close in zip(keys, closes)
            ]

        tops, sums = [None] * HEADS, [None] * HEADS
        ahead = scores_of(*steps[0])
        for index, (head, keys, values, closes) in enumerate(steps):
            scores = ahead
            if index + 1 < len(steps):
                ahead = scores_of(*steps[index + 1])
            if index < HEADS and not fresh_start:
                source = (top_ref, sum_ref) if start is None else start
                tops[head], sums[head] = source[0][head, 0:1], source[1][head]
            top = jnp.max(functools.reduce(jnp.maximum, scores), axis=0, keepdims=True)
            before = tops[head]
            if before is not None:
                top = jnp.maximum(before, top)
            total = None
            for score, value in zip(scores, values):
                weight = jnp.exp2(score - top)
                high = weight.astype(BF16)
                low = (weight - high.astype(F32)).astype(BF16)
                part = dot(value, high) + dot(value, low)
                total = part if total is None else total + part
            if before is not None:
                total = sums[head] * jnp.exp2(before - top) + total
            tops[head], sums[head] = top, total
        for head in range(HEADS):
            sum_ref[head] = sums[head]
            top_ref[head] = jnp.broadcast_to(tops[head], (8, TOKENS))

    here, there, flipped = [], [], []
    for number, base, flip, turn in places:
        context = context_tile(number, base, flip, turn)
        if flip:
            there.append(context)
            flipped.append(block_tile(number, base))
        elif turn == 0:
            here.append([context, diagonal_tile(number, base)])
        else:
            here.append([context, masked_tile(number, base, flip, turn)])
    if len(there) == 1:
        here[-1] += there
    else:
        here.append(there)
    fold(here, first)
    start = None

    @pl.when(blk >= 4)
    def _():
        fold([flipped], False)

    if last:
        for head in range(HEADS):
            total = sum_ref[head]
            mixed = total[:HEAD_SIZE] / total[HEAD_SIZE : HEAD_SIZE + 1]
            out_ref[0, :, head * HEAD_SIZE : (head + 1) * HEAD_SIZE] = mixed.astype(BF16).T


def attend(block_offset, queries, chunks, places, state, last, token, early=()):
    first = state is None
    top, total = (HEADS, 8, TOKENS), (HEADS, HEAD_SIZE + TAIL, TOKENS)
    if last:
        outs = [shape((1, TOKENS, HEADS * HEAD_SIZE), BF16)]
        scratch = [pltpu.VMEM(top, F32), pltpu.VMEM(total, F32)]
    else:
        outs, scratch = [shape(top, F32), shape(total, F32)], []
    operands = [(block_offset, SMEM)]
    operands += [(a, VMEM) for a in (queries, *chunks, *(() if first else state), *early)]
    return run(
        functools.partial(attend_kernel, places, first, last, len(early)),
        "attend",
        24,
        token,
        outs,
        operands,
        scratch,
        cost=3,
    )


def pages_kernel(places, *refs):
    chunks, (mine_ref, other_ref) = refs[:-2], refs[-2:]
    instance = lax.axis_index("blk") * 2 + lax.axis_index("group")
    other = lax.axis_index("blk") * 2 + 1 - lax.axis_index("group")
    slots = 4 * PAGE_TOKENS
    row = lax.broadcasted_iota(jnp.int32, (slots, TOKENS), 0)
    lane = lax.broadcasted_iota(jnp.int32, (slots, TOKENS), 1)
    wanted = jnp.where(row < 2 * PAGE_TOKENS, instance * 2, other * 2) + row // PAGE_TOKENS % 2
    wanted = jnp.where(row % PAGE_TOKENS == lane % PAGE_TOKENS, wanted, -2).astype(F32)
    for number, base, flip, turn in places:
        source = source_of(flip, turn)
        chunk = chunks[number]
        codes = chunk[base + CHUNK : base + PIECE, :].astype(F32)[0:1]
        chooser = jnp.where(wanted == codes, 1.0, 0.0).astype(BF16)
        for part in range(2):
            start = base + (2 + part) * HEAD_SIZE
            found = dot_t(chooser, chunk[start : start + HEAD_SIZE, :]).astype(BF16)
            for rank in range(2):
                mine_ref[source, rank, part] = found[rank * PAGE_TOKENS : (rank + 1) * PAGE_TOKENS]
                other_ref[source, rank, part] = found[
                    (2 + rank) * PAGE_TOKENS : (3 + rank) * PAGE_TOKENS
                ]


def select_pages(chunks, places, token):
    out = shape((8, 2, 2, PAGE_TOKENS, HEAD_SIZE), BF16)
    return run(
        functools.partial(pages_kernel, places),
        "pages",
        8,
        token,
        [out, out],
        [(a, VMEM) for a in chunks],
    )


def pool_kernel(mine_ref, came_ref, out_ref):
    group = lax.axis_index("group")
    out_ref[:, group] = mine_ref[...]
    out_ref[:, 1 - group] = came_ref[...]


def pool(mine, came, token):
    out = shape((8, 2, 2, 2, PAGE_TOKENS, HEAD_SIZE), BF16)
    return run(pool_kernel, "pool", 4, token, [out], [(mine, VMEM), (came, VMEM)])


def attend_rows(
    length_ref, query_ref, step_ref, cache_ref, attended_ref, score_ref, mixed_ref, waits
):
    count = HEADS * STEPS * ROWS
    query = jnp.concatenate(
        [
            query_ref[0, :, :, h * HEAD_SIZE : (h + 1) * HEAD_SIZE].reshape(STEPS * ROWS, HEAD_SIZE)
            for h in range(HEADS)
        ],
        axis=0,
    )
    scaling = HEAD_SIZE**-0.5

    def row_of(width):
        return lax.broadcasted_iota(jnp.int32, (count, width), 0) % ROWS

    row_wide, row_head = row_of(LEN), row_of(HEAD_SIZE)
    lengths = jnp.zeros((count, LEN), jnp.int32)
    for r in range(ROWS):
        if r % (ROWS // 2) == 0:
            waits[r // (ROWS // 2)].wait()
        score = dot_t(query, cache_ref[0, 0, r])
        if r == 0:
            score_ref[...] = score
        else:
            score_ref[...] = jnp.where(row_wide == r, score, score_ref[...])
        lengths = jnp.where(row_wide == r, length_ref[0, r], lengths)
    live = lax.broadcasted_iota(jnp.int32, (count, LEN), 1) < lengths
    score_old = jnp.where(live, score_ref[...] * scaling, LOW_SCORE)
    new_keys = step_ref[0, :, 0].reshape(STEPS * ROWS, HEAD_SIZE)
    new_values = step_ref[0, :, 1].reshape(STEPS * ROWS, HEAD_SIZE)
    lane = lax.broadcasted_iota(jnp.int32, (count, STEPS * ROWS), 1)
    place = lax.broadcasted_iota(jnp.int32, (count, STEPS * ROWS), 0)
    open_new = (lane % ROWS == place % ROWS) & (lane // ROWS <= place // ROWS % STEPS)
    score_new = jnp.where(open_new, dot_t(query, new_keys) * scaling, LOW_SCORE)
    top = jnp.maximum(
        jnp.max(score_old, axis=1, keepdims=True), jnp.max(score_new, axis=1, keepdims=True)
    )
    weight_old = jnp.where(live, jnp.exp(score_old - top), 0.0)
    weight_new = jnp.where(open_new, jnp.exp(score_new - top), 0.0)
    totals = jnp.sum(weight_old, axis=1, keepdims=True) + jnp.sum(weight_new, axis=1, keepdims=True)
    rounded = weight_old.astype(BF16)
    for r in range(ROWS):
        if r % (ROWS // 2) == 0:
            waits[2 + r // (ROWS // 2)].wait()
        mixed = dot(rounded, cache_ref[0, 1, r])
        if r == 0:
            mixed_ref[...] = mixed
        else:
            mixed_ref[...] = jnp.where(row_head == r, mixed, mixed_ref[...])
    mixed = mixed_ref[...] + dot(weight_new.astype(BF16), new_values)
    attended = (mixed / totals).astype(BF16)
    for h in range(HEADS):
        attended_ref[:, h * HEAD_SIZE : (h + 1) * HEAD_SIZE] = attended[
            h * STEPS * ROWS : (h + 1) * STEPS * ROWS
        ]


TURNS = (2, 1, 3, 0)
ORDER = (0, 2, 1, 3)
SPLIT = 2
WIDTH = QUARTER // SPLIT


def decode_kernel(length_hbm, query_hbm, step_hbm, cache_hbm, weight_hbm, *refs):
    outs = refs[:4]
    length_ref, query_ref, step_ref, cache_ref, weight_ref, own_ref, part_ref = refs[4:11]
    attended_ref, score_ref, mixed_ref, row_sems, cache_sems, weight_sems, out_sems = refs[11:]
    firsts = [
        pltpu.make_async_copy(query_hbm, query_ref, row_sems.at[0]),
        pltpu.make_async_copy(step_hbm, step_ref, row_sems.at[1]),
        pltpu.make_async_copy(length_hbm, length_ref, row_sems.at[2]),
    ]
    waits = []
    for number in range(4):
        rows = pl.ds(number % 2 * (ROWS // 2), ROWS // 2)
        waits.append(
            pltpu.make_async_copy(
                cache_hbm.at[0, number // 2, rows],
                cache_ref.at[0, number // 2, rows],
                cache_sems.at[number],
            )
        )
    y = lax.axis_index("tp") // 4
    copies = []
    for number in range(4 * SPLIT):
        column = (y + ORDER[number // SPLIT]) % 4 * QUARTER + number % SPLIT * WIDTH
        copies.append(
            pltpu.make_async_copy(
                weight_hbm.at[:, pl.ds(pl.multiple_of(column, WIDTH), WIDTH)],
                weight_ref.at[number],
                weight_sems.at[number],
            )
        )
    for copy in firsts + waits + copies:
        copy.start()
    for copy in firsts:
        copy.wait()
    attend_rows(
        length_ref, query_ref, step_ref, cache_ref, attended_ref, score_ref, mixed_ref, waits
    )
    attended = attended_ref[...]
    leaving = []
    for number, copy in enumerate(copies):
        copy.wait()
        part = dot(attended, weight_ref[number])
        quarter = number // SPLIT
        columns = slice(number % SPLIT * WIDTH, (number % SPLIT + 1) * WIDTH)
        if quarter == 0:
            own_ref[:, columns] = part
        else:
            part_ref[quarter - 1, :, columns] = part.astype(BF16)
        if number % SPLIT == SPLIT - 1:
            source = own_ref if quarter == 0 else part_ref.at[quarter - 1]
            leaving.append(pltpu.make_async_copy(source, outs[quarter], out_sems.at[quarter]))
            leaving[-1].start()
    for copy in leaving:
        copy.wait()


def decode(row_lengths, step_query, step_cache, row_cache, out_weight):
    rows = STEPS * ROWS
    operands = (row_lengths, step_query, step_cache, row_cache, out_weight)
    return run(
        decode_kernel,
        "decode",
        58,
        None,
        [shape((rows, QUARTER), BF16 if turn else F32) for turn in ORDER],
        [(a, pl.ANY) for a in operands],
        [
            pltpu.SMEM((1, ROWS), jnp.int32),
            pltpu.VMEM(step_query.shape, BF16),
            pltpu.VMEM(step_cache.shape, BF16),
            pltpu.VMEM(row_cache.shape, BF16),
            pltpu.VMEM((4 * SPLIT, out_weight.shape[0], WIDTH), BF16),
            pltpu.VMEM((rows, QUARTER), F32),
            pltpu.VMEM((3, rows, QUARTER), BF16),
            pltpu.VMEM((rows, HEADS * HEAD_SIZE), BF16),
            pltpu.VMEM((HEADS * rows, LEN), F32),
            pltpu.VMEM((HEADS * rows, HEAD_SIZE), F32),
            pltpu.SemaphoreType.DMA((3,)),
            pltpu.SemaphoreType.DMA((4,)),
            pltpu.SemaphoreType.DMA((4 * SPLIT,)),
            pltpu.SemaphoreType.DMA((4,)),
        ],
        cost=9,
        emit=False,
        space=pl.ANY,
    )


def quarter_kernel(own_ref, a_ref, b_ref, c_ref, *outs):
    z = lax.axis_index("tp") % 4
    for out, turn in zip(outs, TURNS):
        columns = pl.ds(pl.multiple_of((z + turn) % 4 * SHARE, SHARE), SHARE)
        total = (
            own_ref[:, columns]
            + a_ref[:, columns].astype(F32)
            + b_ref[:, columns].astype(F32)
            + c_ref[:, columns].astype(F32)
        )
        out[...] = total.astype(out.dtype)


def sum_quarters(own, came, token):
    outs = [shape((STEPS * ROWS, SHARE), BF16 if turn == 2 else F32) for turn in TURNS]
    operands = [(a, VMEM) for a in (own, *came)]
    return run(quarter_kernel, "quarters", 4, token, outs, operands, cost=4)


def diagonal():
    rows = lax.broadcasted_iota(jnp.int32, (STEPS * ROWS, HEAD_SIZE), 0)
    return rows == lax.broadcasted_iota(jnp.int32, (STEPS * ROWS, HEAD_SIZE), 1)


def hidden_kernel(residual_ref, own_ref, a_ref, b_ref, c_ref, hidden_ref, square_ref):
    residual = residual_ref[0].reshape(STEPS * ROWS, SHARE).astype(F32)
    hidden = residual + (
        own_ref[...] + a_ref[...].astype(F32) + b_ref[...] + c_ref[...]
    )
    hidden_ref[...] = hidden
    square = jnp.sum(hidden * hidden, axis=1, keepdims=True)
    square = jnp.sum(jnp.where(diagonal(), square, 0.0), axis=0, keepdims=True)
    square_ref[...] = jnp.broadcast_to(square[None], square_ref.shape)


def sum_shares(residual, own, came, token):
    outs = [shape((STEPS * ROWS, SHARE), F32), shape((16, 1, HEAD_SIZE), F32)]
    operands = [(a, VMEM) for a in (residual, own, *came)]
    return run(hidden_kernel, "hidden", 4, token, outs, operands, cost=4)


def finish_kernel(hidden_ref, gain_ref, square_ref, out_ref):
    square = jnp.sum(square_ref[...], axis=0)
    square = jnp.sum(jnp.where(diagonal(), square, 0.0), axis=1, keepdims=True)
    scale = lax.rsqrt(square * (1.0 / COLUMNS) + EPSILON)
    out = hidden_ref[...] * scale * gain_ref[...].reshape(1, SHARE).astype(F32)
    out_ref[0] = out.astype(BF16).reshape(STEPS, ROWS, SHARE)


def finish(hidden, gain, squares, token):
    outs = [shape((1, STEPS, ROWS, SHARE), BF16)]
    operands = [(a, VMEM) for a in (hidden, gain, squares)]
    return run(finish_kernel, "finish", 4, token, outs, operands)


def move_x(a, turn):
    return lax.ppermute(a, "blk", [(i, i // 4 * 4 + (i + turn) % 4) for i in range(8)])


def move_y(a, turn):
    return lax.ppermute(a, "tp", [(i, (i + 4 * turn) % 16) for i in range(16)])


def move_z(a, turn):
    return lax.ppermute(a, "tp", [(i, i // 4 * 4 + (i + turn) % 4) for i in range(16)])


def body(
    prompt_query,
    context_cache,
    new_block_cache,
    block_offset,
    page_owner,
    step_query,
    step_cache,
    row_cache,
    row_lengths,
    out_weight,
    residual,
    norm_gain,
):
    packed = pack(
        page_owner.reshape(1, PAGES),
        jnp.swapaxes(context_cache, 2, 3),
        jnp.swapaxes(new_block_cache, 2, 3),
    )
    near = lax.ppermute(packed, "tp", [(i, i ^ 1) for i in range(16)])
    far = lax.ppermute(packed, "blk", [(i, i ^ 4) for i in range(8)])
    own, *parts = decode(row_lengths, step_query, step_cache, row_cache, out_weight)
    far, parts[0] = lax.optimization_barrier((far, parts[0]))
    far_near = lax.ppermute(far, "tp", [(i, i ^ 1) for i in range(16)])
    came = [move_y(a, turn) for a, turn in zip(parts, TURNS)]
    here, token = join(packed, near, far, far_near, None)
    up = move_x(here, 1)
    down = move_x(here, 3)
    *state, token = attend(
        block_offset,
        prompt_query,
        [here],
        [(0, 0, 0, 0), (0, PIECE, 1, 0)],
        None,
        False,
        token,
        [own],
    )
    *shares, own, token = sum_quarters(own, came, token)
    came = [move_z(a, turn) for a, turn in zip(shares, TURNS)]
    places = [(0, 0, 0, -1), (0, PIECE, 1, -1)]
    *state, token = attend(block_offset, prompt_query, [up], places, state, False, token)
    up_two, down_two, token = relay(up, down, token)
    up_two = move_x(up_two, 1)
    down_two = move_x(down_two, 3)
    hidden, square, token = sum_shares(residual, own, came, token)
    squares = lax.all_to_all(square, "tp", split_axis=0, concat_axis=0, tiled=True)
    places = [(0, 0, 0, 0), (0, PIECE, 1, 0), (1, 0, 0, -1), (1, PIECE, 1, -1)]
    places += [(2, 0, 0, 1), (2, PIECE, 1, 1), (3, 0, 0, 2), (4, 0, 1, 2)]
    mine, other, token = select_pages([here, up, down, up_two, down_two], places, token)
    other = lax.ppermute(other, "group", [(0, 1), (1, 0)])
    prefill_out, token = attend(
        block_offset,
        prompt_query,
        [down, up_two, down_two],
        [(0, 0, 0, 1), (0, PIECE, 1, 1), (1, 0, 0, 2), (2, 0, 1, 2)],
        state,
        True,
        token,
    )
    page_pool, token = pool(mine, other, token)
    decode_out, token = finish(hidden, norm_gain, squares, token)
    return (prefill_out, page_pool.reshape(1, 32, 2, PAGE_TOKENS, HEAD_SIZE), decode_out)


def solution(mesh):
    placed = (
        P("group", "blk", "tp"),
        P("group", None, "blk", "tp"),
        P("group", None, "blk", "tp"),
        P(),
        P("group", "blk", None),
        P(("blk", "group"), None, None, "tp"),
        P(("blk", "group"), None, None, None, "tp"),
        P(("blk", "group"), None, None, None, "tp"),
        P(("blk", "group"), None),
        P("tp", None),
        P(("blk", "group"), None, None, "tp"),
        P("tp"),
    )
    return jax.shard_map(
        body,
        mesh=mesh,
        in_specs=placed,
        out_specs=(
            P("group", "blk", "tp"),
            P(("blk", "group"), None, None, None, "tp"),
            P(("blk", "group"), None, None, "tp"),
        ),
        check_vma=False,
    )
```
